128 devices in a mesh: rows: 32 (over z, y, core), vecs: 4 (over x).
Axes of the slice: x: 4, y: 4, z: 4, core: 2. Of those that a mesh axis runs over, the one named last changes fastest.
Arguments:
- vectors: bfloat16 [131072, 1024], P('rows', 'vecs'), may hold values from -6 to 6, as said below
- blocks: bfloat16 [1024, 5, 128, 128], P('rows'), may hold values from -0.25 to 0.25
- columns: int32 [1024, 5], P('rows'), may hold values from 0 to 1023, as said below
Outputs:
- basis: float32 [131072, 1024], P('rows', 'vecs')
The draws below stay inside these ranges and needn't reach their ends.
Inputs may be any that keep to these rules, and one draw needn't show every extreme that they name: Each block row i names 5 block columns of the form i + d clipped to 0 .. 1023, with distinct d in -8 .. 8; near the grid's ends some may repeat. `vectors`: entries of order one.
All inputs are finite; a program needn't handle non-finite values.
Results may differ from the reference program's by a relative error of at most 0.0075.
Values may be sent and summed in bfloat16 or wider, within the bound.
No kernel may reach another device: no remote copies, remote signals or barrier semaphores. Data moves between devices by JAX's collectives and lax.ppermute only.
A program may use at most 128 MiB of HBM per device.

```python
import jax
import jax.numpy as jnp
from jax import lax

B = 128
K = 1024
NNZ = 5
DEGREE = 4
BR_DEV = 32
REACH = 8
NB = 1024
NROWS = 131072
N_ROWS = 32


def draw_columns(key, part):
    breadth = 2 * REACH + 1
    row_ids = jnp.arange(NB, dtype=jnp.int32)[:, None]
    scores = jax.random.randint(key, (NB, breadth), 0, 1 << 20, dtype=jnp.int32) * breadth + jnp.arange(breadth, dtype=jnp.int32)[None, :]
    values, chosen = lax.top_k(scores, NNZ)
    picked = jnp.clip(row_ids + chosen.astype(jnp.int32) - REACH, 0, NB - 1)
    return picked.astype(jnp.int32)


def draw_vectors(key, part):
    first_key = jax.random.fold_in(key, 11)
    third_key = jax.random.fold_in(key, 13)
    entries = jax.random.normal(first_key, (NROWS, K), jnp.float32)
    common = jax.random.normal(third_key, (NROWS, 1), jnp.float32)
    values = jnp.clip(entries + 0.4 * common, -6.0, 6.0)
    return values.astype(jnp.bfloat16)


def block_scale(rng, shape, shards, smallest, largest):
    loudness = 1.0
    for axis_at, shards_of in shards:
        draws = jax.random.uniform(jax.random.fold_in(jax.random.fold_in(rng, 6), axis_at), (shards_of,), jnp.float32, smallest / len(shards), largest / len(shards))
        loudness = loudness * jnp.repeat(jnp.exp(draws), shape[axis_at] // shards_of).reshape((-1,) + (1,) * (len(shape) - 1 - axis_at))
    return loudness


def bell_draw(key, shape, width, reach, shards=(), held_as=jnp.bfloat16):
    level = block_scale(key, shape, shards, -0.22, 0.18) if shards else 1.0
    values = jax.random.normal(key, shape, jnp.float32) * width * level
    return jnp.minimum(jnp.maximum(values, -reach), reach).astype(held_as)


def setup_inputs(seed: int = 0) -> dict:
    splits = jax.random.split(jax.random.key(seed), 4)
    vectors = draw_vectors(jax.random.fold_in(splits[3], 71), 0)
    blocks = bell_draw(splits[1], (NB, NNZ, B, B), (NNZ * B) ** -0.5, 0.25, ((0, 32),))
    columns = draw_columns(jax.random.fold_in(splits[3], 71), 0)
    return dict(vectors=vectors, blocks=blocks, columns=columns)


filter_center = 0.25
filter_radius = 1.25

def product(vec_bf, blocks, columns):
    stacked = vec_bf.reshape(NB, B, K)
    cols_slab = columns.reshape(N_ROWS, BR_DEV, NNZ)
    blocks_slab = blocks.reshape(N_ROWS, BR_DEV, NNZ, B, B)

    def one_slab(pair):
        slab_cols, slab_blocks = pair
        picked = stacked[slab_cols].astype(jnp.float32)
        return jnp.einsum('rjab,rjbk->rak', slab_blocks.astype(jnp.float32), picked)
    result = lax.map(one_slab, (cols_slab, blocks_slab))
    return result.reshape(NROWS, K)

def reference(vectors, blocks, columns):
    older = vectors.astype(jnp.float32)
    current = (product(vectors, blocks, columns) - filter_center * older) / filter_radius
    for iteration in range(1, DEGREE):
        rounded = current.astype(jnp.bfloat16)
        newer = 2.0 * (product(rounded, blocks, columns) - filter_center * current) / filter_radius - older
        older = current
        current = newer
    final = current.astype(jnp.bfloat16)
    gram_matrix = jnp.dot(final.T.astype(jnp.float32), final.astype(jnp.float32), preferred_element_type=jnp.float32) / NROWS
    lower = jnp.linalg.cholesky(gram_matrix)
    identity = jnp.eye(K, dtype=jnp.float32)
    inverse = lax.linalg.triangular_solve(lower, identity, left_side=True, lower=True)
    inverse_high = inverse.astype(jnp.bfloat16)
    inverse_low = (inverse - inverse_high.astype(jnp.float32)).astype(jnp.bfloat16)
    first = jnp.dot(final.astype(jnp.float32), inverse_high.T.astype(jnp.float32), preferred_element_type=jnp.float32)
    second = jnp.dot(final.astype(jnp.float32), inverse_low.T.astype(jnp.float32), preferred_element_type=jnp.float32)
    return first + second
```

```python
import functools

import jax
import jax.numpy as jnp
from jax import lax
from jax.experimental import pallas as pl
from jax.experimental.pallas import tpu as pltpu
from jax.sharding import PartitionSpec as P

DEGREE = 4
filter_center = 0.25
filter_radius = 1.25

F32 = jnp.float32
BF = jnp.bfloat16
EXACT = lax.Precision.HIGHEST
SIZE = 128
REACH = 8
MIB = 1 << 20

ANY = pl.BlockSpec(memory_space=pl.ANY)


def params(mib):
    return pltpu.CompilerParams(vmem_limit_bytes=mib * MIB)


def load_all(pairs, sems):
    copies = [pltpu.make_async_copy(src, dst, sems.at[n]) for n, (src, dst) in enumerate(pairs)]
    for copy in copies:
        copy.start()
    for copy in copies:
        copy.wait()


def row_product(idx, row, shift, blocks_ref, r, pad):
    count = blocks_ref.shape[1]
    left = jnp.concatenate([blocks_ref[r, j] for j in range(count)], axis=1)
    right = jnp.concatenate([pad[idx[row, j] - shift] for j in range(count)], axis=0)
    return jnp.dot(left, right, preferred_element_type=F32)


def recurrence(step, product, current, older):
    scale = (2.0 if step else 1.0) / filter_radius
    newer = scale * product - (scale * filter_center) * current.astype(F32)
    return newer - older.astype(F32) if step else newer


def edge_kernel(step, last, offsets, idx, place, *refs):
    refs = list(refs)
    take = lambda n: [refs.pop(0) for _ in range(n)]
    blocks = take(2)
    before, low, mid, high, after = take(5)
    current = take(2)
    older = take(2) if step else [None, None]
    if last:
        (mid_new,) = take(1)
        sends = take(4)
        pad, sems, final_low, final_high, out_sems = take(5)
        rounded = [final_low, final_high]
    else:
        fresh = take(2)
        rounded = take(2)
        pad, sems = take(2)
    g = pl.program_id(0)
    per = blocks[0].shape[0]

    @pl.when(g == 0)
    def _():
        load_all(
            [
                (before, pad.at[pl.ds(0, 8)]),
                (low.at[pl.ds(offsets[0], 8)], pad.at[pl.ds(8, 8)]),
                (mid.at[pl.ds(offsets[1], 16)], pad.at[pl.ds(16, 16)]),
                (high.at[pl.ds(offsets[2], 8)], pad.at[pl.ds(32, 8)]),
                (after, pad.at[pl.ds(40, 8)]),
            ],
            sems,
        )

    for side in range(2):
        for r in range(per):
            row = 24 * side + g * per + r
            product = row_product(idx, row, 0, blocks[side], r, pad)
            old = older[side][r] if step else None
            newer = recurrence(step, product, current[side][r], old)
            if last:
                rounded[side][g * per + r] = newer.astype(BF)
            else:
                fresh[side][r] = newer
                rounded[side][r] = newer.astype(BF)

    if last:

        @pl.when(g == pl.num_programs(0) - 1)
        def _():
            sources = [final_low, mid_new.at[pl.ds(0, 8)], mid_new.at[pl.ds(8, 8)], final_high]
            for s in range(4):
                for q in range(4):

                    @pl.when(lax.rem(place[0] + s, 4) == q)
                    def _():
                        pltpu.make_async_copy(sources[q], sends[s], out_sems.at[s]).start()

            for s in range(4):
                pltpu.make_async_copy(final_low, sends[s], out_sems.at[s]).wait()


def middle_kernel(step, last, offsets, idx, *refs):
    refs = list(refs)
    take = lambda n: [refs.pop(0) for _ in range(n)]
    (blocks,) = take(1)
    low, mid, high = take(3)
    (current,) = take(1)
    older = take(1)[0] if step else None
    fresh = None if last else take(1)[0]
    rounded, pad, sems = take(3)
    g = pl.program_id(0)
    per = blocks.shape[0]

    @pl.when(g == 0)
    def _():
        load_all(
            [
                (low.at[pl.ds(offsets[0], 8)], pad.at[pl.ds(0, 8)]),
                (mid.at[pl.ds(offsets[1], 16)], pad.at[pl.ds(8, 16)]),
                (high.at[pl.ds(offsets[2], 8)], pad.at[pl.ds(24, 8)]),
            ],
            sems,
        )

    for r in range(per):
        product = row_product(idx, 8 + g * per + r, 8, blocks, r, pad)
        newer = recurrence(step, product, current[r], older[r] if step else None)
        if not last:
            fresh[r] = newer
        rounded[r] = newer.astype(BF)


def spec_rows(per, width, first):
    return pl.BlockSpec((per, SIZE, width), lambda g, *_: (g + first // per, 0, 0))


def filter_edges(step, last, idx, place, blocks, halo, rounded, current, older, mid_new):
    width = rounded[0][0].shape[-1]
    per = 2
    nnz = blocks.shape[1]
    block_spec = lambda first: pl.BlockSpec((per, nnz, SIZE, SIZE), lambda g, *_: (g + first // per, 0, 0, 0))
    in_specs = [block_spec(0), block_spec(24)] + [ANY] * 5
    operands = [blocks, blocks, halo[0], rounded[0][0], rounded[1][0], rounded[2][0], halo[1]]
    for group in [current] + ([older] if step else []):
        for piece in (0, 2):
            in_specs.append(spec_rows(per, width, group[piece][1]))
            operands.append(group[piece][0])
    scratch = [pltpu.VMEM((48, SIZE, width), BF), pltpu.SemaphoreType.DMA((5,))]
    if last:
        in_specs.append(ANY)
        operands.append(mid_new)
        out_shape = [jax.ShapeDtypeStruct((8, SIZE, width), BF)] * 4
        out_specs = [ANY] * 4
        scratch += [pltpu.VMEM((8, SIZE, width), BF)] * 2 + [pltpu.SemaphoreType.DMA((4,))]
    else:
        out_shape = [jax.ShapeDtypeStruct((8, SIZE, width), F32)] * 2 + [jax.ShapeDtypeStruct((8, SIZE, width), BF)] * 2
        out_specs = [spec_rows(per, width, 0)] * 4
    offsets = tuple(piece[1] for piece in rounded)
    return pl.pallas_call(
        functools.partial(edge_kernel, step, last, offsets),
        out_shape=out_shape,
        grid_spec=pltpu.PrefetchScalarGridSpec(
            num_scalar_prefetch=2,
            grid=(8 // per,),
            in_specs=in_specs,
            out_specs=out_specs,
            scratch_shapes=scratch,
        ),
        compiler_params=params(24),
        cost_estimate=pl.CostEstimate(flops=16 * 5 * 2 * 128 * 128 * 256, bytes_accessed=12 * MIB, transcendentals=0),
        name="filter_edges",
    )(idx, place, *operands)


def filter_middle(step, last, idx, blocks, rounded, current, older):
    width = rounded[0][0].shape[-1]
    per = 4
    nnz = blocks.shape[1]
    in_specs = [pl.BlockSpec((per, nnz, SIZE, SIZE), lambda g, *_: (g + 8 // per, 0, 0, 0))] + [ANY] * 3
    operands = [blocks] + [piece[0] for piece in rounded]
    for group in [current] + ([older] if step else []):
        in_specs.append(spec_rows(per, width, group[1][1]))
        operands.append(group[1][0])
    out_shape = [jax.ShapeDtypeStruct((16, SIZE, width), F32), jax.ShapeDtypeStruct((16, SIZE, width), BF)]
    if last:
        out_shape = out_shape[1:]
    offsets = tuple(piece[1] for piece in rounded)
    return pl.pallas_call(
        functools.partial(middle_kernel, step, last, offsets),
        out_shape=out_shape,
        grid_spec=pltpu.PrefetchScalarGridSpec(
            num_scalar_prefetch=1,
            grid=(16 // per,),
            in_specs=in_specs,
            out_specs=[spec_rows(per, width, 0)] * len(out_shape),
            scratch_shapes=[pltpu.VMEM((32, SIZE, width), BF), pltpu.SemaphoreType.DMA((3,))],
        ),
        compiler_params=params(24),
        cost_estimate=pl.CostEstimate(flops=16 * 5 * 2 * 128 * 128 * 256, bytes_accessed=12 * MIB, transcendentals=0),
        name="filter_middle",
    )(idx, *operands)


def exchange_halo(low, high):
    count = lax.axis_size("rows")
    up = [(i, i + 1) for i in range(count - 1)]
    down = [(j, i) for i, j in up]
    return lax.ppermute(high, "rows", up), lax.ppermute(low, "rows", down)


PAIRS = [(a, b) for a in range(4) for b in range(a, 4)]
HALF = len(PAIRS) // 2


def gram_kernel(total_rows, place, own, got1, got2, got3, keep, send, stacked, f, g, sems, out_sems):
    pieces = [own, got1, got2, got3]
    x, core = place[0], place[1]
    load_all([(pieces[s], f.at[lax.rem(x + 4 - s, 4)]) for s in range(4)], sems)
    copy_f = pltpu.make_async_copy(f, stacked, out_sems.at[2])
    copy_f.start()
    depth = 8 * SIZE
    width = f.shape[-1]
    for a in range(4):
        left = f[a].reshape(depth, width).T
        for b in range(a, 4):
            n = PAIRS.index((a, b))
            tile = jnp.dot(left, f[b].reshape(depth, width), preferred_element_type=F32) * (1.0 / total_rows)
            for r in range(2):
                for c in range(2):
                    g[n // HALF, n % HALF, r, c] = tile[r * SIZE : (r + 1) * SIZE, c * SIZE : (c + 1) * SIZE]
    copy_keep = pltpu.make_async_copy(g.at[core], keep, out_sems.at[0])
    copy_send = pltpu.make_async_copy(g.at[1 - core], send, out_sems.at[1])
    copy_keep.start()
    copy_send.start()
    copy_keep.wait()
    copy_send.wait()
    copy_f.wait()


def gram(total_rows, place, own, got):
    width = own.shape[-1]
    half = jax.ShapeDtypeStruct((HALF, 2, 2, SIZE, SIZE), F32)
    return pl.pallas_call(
        functools.partial(gram_kernel, total_rows),
        out_shape=[half, half, jax.ShapeDtypeStruct((4, 8, SIZE, width), BF)],
        grid_spec=pltpu.PrefetchScalarGridSpec(
            num_scalar_prefetch=1,
            grid=(),
            in_specs=[ANY] * 4,
            out_specs=[ANY] * 3,
            scratch_shapes=[
                pltpu.VMEM((4, 8, SIZE, width), BF),
                pltpu.VMEM((2, HALF, 2, 2, SIZE, SIZE), F32),
                pltpu.SemaphoreType.DMA((4,)),
                pltpu.SemaphoreType.DMA((3,)),
            ],
        ),
        compiler_params=params(24),
        cost_estimate=pl.CostEstimate(flops=10 * 2 * 1024 * 256 * 256, bytes_accessed=8 * MIB, transcendentals=0),
        name="gram",
    )(place, own, *got)


def sum_everywhere(keep, send):
    rows = lax.axis_size("rows")
    vecs = lax.axis_size("vecs")
    swap = [(i, i ^ 1) for i in range(rows)]
    groups = [list(range(c, rows, 2)) for c in range(2)]
    count = rows // 2
    mine = keep + lax.ppermute(send, "rows", swap)
    parts = mine.reshape(count, -1, SIZE)
    parts = lax.all_to_all(parts, "rows", 0, 0, axis_index_groups=groups, tiled=True)
    part = jnp.sum(parts, axis=0)
    others = [lax.ppermute(part, "vecs", [(i, (i + s) % vecs) for i in range(vecs)]) for s in range(1, vecs)]
    part = part + sum(others)
    spread_out = jnp.broadcast_to(part[None], (count,) + part.shape)
    mine = lax.all_to_all(spread_out, "rows", 0, 0, axis_index_groups=groups, tiled=True).reshape(keep.shape)
    return mine, lax.ppermute(mine, "rows", swap)


def recip(x):
    y = pl.reciprocal(x, approx=True)
    return y * (2.0 - x * y)


def inv_sqrt(x):
    y = lax.rsqrt(x)
    return y * (1.5 - 0.5 * x * (y * y))


def spread(x):
    return jnp.broadcast_to(x, (8, SIZE))


def eliminate(rows):
    count = len(rows)
    lane = lax.broadcasted_iota(jnp.int32, (8, SIZE), 1)
    sub = lax.broadcasted_iota(jnp.int32, (8, SIZE), 0)
    done = []
    for k in range(count):
        base = 8 * k
        inside = (lane >= base) & (lane < base + 8)
        cols = {(q, i): spread(rows[i][:, base + q : base + q + 1]) for i in range(k, count) for q in range(8)}
        s = {(r, q): spread(cols[q, k][r : r + 1, :]) for r in range(8) for q in range(r + 1)}
        own = jnp.where(inside, jnp.where(lane == base + sub, 1.0, 0.0), rows[k])
        row = [spread(own[q : q + 1, :]) for q in range(8)]
        inv = {}
        m = {}
        for j in range(8):
            inv[j] = recip(s[j, j])
            for i in range(j + 1, 8):
                m[i, j] = s[i, j] * inv[j]
            for i in range(j + 1, 8):
                for t in range(j + 1, i + 1):
                    s[i, t] = s[i, t] - m[i, j] * s[t, j]
                row[i] = row[i] - m[i, j] * row[j]
        out = None
        for p in range(8):
            scaled = row[p] * inv_sqrt(s[p, p])
            out = scaled if out is None else jnp.where(sub == p, scaled, out)
        done.append(jnp.where(lane <= base + sub, out, 0.0))
        z = [row[p] * inv[p] for p in range(8)]
        for q in range(6, -1, -1):
            for p in range(7, q, -1):
                z[q] = z[q] - m[p, q] * z[p]
        for i in range(k + 1, count):
            total = jnp.where(inside, 0.0, rows[i])
            for q in range(8):
                total = total - cols[q, i] * z[q]
            rows[i] = total
    return done


def factor_kernel(place, mine, other, high_ref, low_ref, w, panel, diag, sems):
    n = w.shape[0]
    x, core = place[0], place[1]

    def copies(halves):
        return [
            pltpu.make_async_copy(
                halves[m // HALF].at[m % HALF], w.at[pl.ds(2 * a, 2), pl.ds(2 * b, 2)], sems.at[m]
            )
            for m, (a, b) in enumerate(PAIRS)
        ]

    @pl.when(core == 0)
    def _():
        for copy in copies([mine, other]):
            copy.start()

    @pl.when(core == 1)
    def _():
        for copy in copies([other, mine]):
            copy.start()

    for copy in copies([mine, other]):
        copy.wait()

    def step(k, _):
        done = eliminate([w[k, k, pl.ds(8 * r, 8), :] for r in range(16)])
        for r in range(16):
            diag[pl.ds(8 * r, 8), :] = done[r]
        inverse = diag[...]
        for c in range(n):
            panel[c] = jnp.dot(inverse, w[k, c], preferred_element_type=F32, precision=EXACT)
        panel[k] = inverse
        for c in range(n):
            w[k, c] = panel[c]

        def below(i, _):
            w[i, k] = jnp.zeros((SIZE, SIZE), F32)
            left = panel[i].T
            for c in range(n):
                w[i, c] = w[i, c] - jnp.dot(left, panel[c], preferred_element_type=F32, precision=EXACT)
            return 0

        lax.fori_loop(k + 1, n, below, 0)
        return 0

    for i in range(n):
        for c in range(i - i % 2):
            w[i, c] = jnp.zeros((SIZE, SIZE), F32)
    lax.fori_loop(0, n, step, 0)
    for r in range(2):
        for c in range(n):
            i = 2 * x + r
            value = jnp.where(c <= i, w[i, c], 0.0)
            high = value.astype(BF)
            high_ref[pl.ds(SIZE * r, SIZE), pl.ds(SIZE * c, SIZE)] = high
            low_ref[pl.ds(SIZE * r, SIZE), pl.ds(SIZE * c, SIZE)] = (value - high.astype(F32)).astype(BF)


def factor(place, mine, other):
    n = 8
    vmem = pl.BlockSpec(memory_space=pltpu.VMEM)
    return pl.pallas_call(
        factor_kernel,
        out_shape=[jax.ShapeDtypeStruct((2 * SIZE, n * SIZE), BF)] * 2,
        grid_spec=pltpu.PrefetchScalarGridSpec(
            num_scalar_prefetch=1,
            grid=(),
            in_specs=[ANY] * 2,
            out_specs=[vmem] * 2,
            scratch_shapes=[
                pltpu.VMEM((n, n, SIZE, SIZE), F32),
                pltpu.VMEM((n, SIZE, SIZE), F32),
                pltpu.VMEM((SIZE, SIZE), F32),
                pltpu.SemaphoreType.DMA((len(PAIRS),)),
            ],
        ),
        compiler_params=params(24),
        cost_estimate=pl.CostEstimate(flops=80_000_000_000, bytes_accessed=4 * MIB, transcendentals=0),
        name="factor",
    )(place, mine, other)


def apply_kernel(place, f0, f1, f2, f3, high, low, out):
    x = place[0]
    t = pl.program_id(0)
    per = f0.shape[1]
    width = f0.shape[-1]
    dims = (((1,), (1,)), ((), ()))
    for s, f in enumerate((f0, f1, f2, f3)):
        quarter = lax.rem(x + 4 - s, 4)
        left = jnp.concatenate([f[p].reshape(per * SIZE, width) for p in range(4)], axis=1)
        value = lax.dot_general(left, high[...], dims, preferred_element_type=F32)
        value = value + lax.dot_general(left, low[...], dims, preferred_element_type=F32)
        out[quarter, pl.ds(t * per, per)] = value.reshape(per, SIZE, width)


def apply(place, pieces, high, low):
    width = pieces[0].shape[-1]
    per = 2
    whole = pl.BlockSpec(high.shape, lambda t, *_: (0, 0))
    return pl.pallas_call(
        apply_kernel,
        out_shape=jax.ShapeDtypeStruct((4, 8, SIZE, width), F32),
        grid_spec=pltpu.PrefetchScalarGridSpec(
            num_scalar_prefetch=1,
            grid=(8 // per,),
            in_specs=[pl.BlockSpec((4, per, SIZE, width), lambda t, *_: (0, t, 0, 0))] * 4 + [whole, whole],
            out_specs=pl.BlockSpec((4, 8, SIZE, width), lambda t, *_: (0, 0, 0, 0)),
        ),
        compiler_params=params(32),
        cost_estimate=pl.CostEstimate(flops=4 * 1024 * 1024 * 256 * 4, bytes_accessed=14 * MIB, transcendentals=0),
        name="apply",
    )(place, *pieces, high, low)


def shards(vectors, blocks, columns):
    block_rows = blocks.shape[0]
    width = vectors.shape[1]
    row = lax.axis_index("rows")
    x = lax.axis_index("vecs")
    vecs = lax.axis_size("vecs")
    total_rows = vectors.shape[0] * lax.axis_size("rows")
    idx = columns - row * block_rows + REACH
    place = jnp.stack([x, lax.rem(row, 2)]).astype(jnp.int32)
    start = vectors.reshape(block_rows, SIZE, width)
    older = None
    current = rounded = [(start, 0), (start, 8), (start, 24)]
    low, high = start[:8], start[24:]
    for step in range(DEGREE):
        last = step == DEGREE - 1
        halo = exchange_halo(low, high)
        middle = filter_middle(step, last, idx, blocks, rounded, current, older)
        mid_new = middle[-1]
        edges = filter_edges(step, last, idx, place, blocks, halo, rounded, current, older, mid_new)
        if not last:
            fresh_low, fresh_high, low, high = edges
            older = current
            current = [(fresh_low, 0), (middle[0], 0), (fresh_high, 0)]
            rounded = [(low, 0), (mid_new, 0), (high, 0)]
    shift = lambda a, s: lax.ppermute(a, "vecs", [(i, (i + s) % vecs) for i in range(vecs)])
    got = [shift(edges[s], s) for s in range(1, vecs)]
    keep, send, quarter = gram(total_rows, place, edges[0], got)
    mine, other = sum_everywhere(keep, send)
    quarter, mine, other = lax.optimization_barrier((quarter, mine, other))
    pieces = [quarter] + [shift(quarter, s) for s in range(1, vecs)]
    inverse_high, inverse_low = factor(place, mine, other)
    return apply(place, pieces, inverse_high, inverse_low).reshape(vectors.shape)


def solution(mesh):
    in_specs = (P("rows", "vecs"), P("rows", None, None, None), P("rows", None))
    out_specs = P("rows", "vecs")
    return jax.shard_map(shards, mesh=mesh, in_specs=in_specs, out_specs=out_specs, check_vma=False)
```

```python
import functools

import jax
import jax.numpy as jnp
from jax import lax
from jax.experimental import pallas as pl
from jax.experimental.pallas import tpu as pltpu
from jax.sharding import PartitionSpec as P

DEGREE = 4
filter_center = 0.25
filter_radius = 1.25

F32 = jnp.float32
BF = jnp.bfloat16
EXACT = lax.Precision.HIGHEST
SIZE = 128
REACH = 8
MIB = 1 << 20

ANY = pl.BlockSpec(memory_space=pl.ANY)


def params(mib):
    return pltpu.CompilerParams(vmem_limit_bytes=mib * MIB)


def load_all(pairs, sems):
    copies = [pltpu.make_async_copy(src, dst, sems.at[n]) for n, (src, dst) in enumerate(pairs)]
    for copy in copies:
        copy.start()
    for copy in copies:
        copy.wait()


def row_product(idx, row, shift, blocks_ref, r, pad):
    count = blocks_ref.shape[1]
    left = jnp.concatenate([blocks_ref[r, j] for j in range(count)], axis=1)
    right = jnp.concatenate([pad[idx[row, j] - shift] for j in range(count)], axis=0)
    return jnp.dot(left, right, preferred_element_type=F32)


def recurrence(step, product, current, older):
    scale = (2.0 if step else 1.0) / filter_radius
    newer = scale * product - (scale * filter_center) * current.astype(F32)
    return newer - older.astype(F32) if step else newer


def far_kernel(step, last, source_at, idx, place, *refs):
    refs = list(refs)
    take = lambda n: [refs.pop(0) for _ in range(n)]
    (blocks,) = take(1)
    halo, far, mid = take(3)
    (current,) = take(1)
    older = take(1)[0] if step else None
    if last:
        near_new, mid_new = take(2)
        sends = take(4)
        pad, sems, rounded, out_sems = take(4)
    else:
        fresh, rounded = take(2)
        pad, sems = take(2)
    g = pl.program_id(0)
    per = blocks.shape[0]
    core = place[1]
    far_at = 24 * core if source_at else 0
    mid_at = 8 if source_at else 0

    @pl.when(g == 0)
    def _():
        load_all(
            [
                (halo, pad.at[pl.ds(16 * core, 8)]),
                (far.at[pl.ds(far_at, 8)], pad.at[pl.ds(8, 8)]),
                (mid.at[pl.ds(mid_at + 8 * core, 8)], pad.at[pl.ds(16 * (1 - core), 8)]),
            ],
            sems,
        )

    for r in range(per):
        product = row_product(idx, 24 * core + g * per + r, 24 * core, blocks, r, pad)
        newer = recurrence(step, product, current[r], older[r] if step else None)
        if last:
            rounded[g * per + r] = newer.astype(BF)
        else:
            fresh[r] = newer
            rounded[r] = newer.astype(BF)

    if last:

        @pl.when(g == pl.num_programs(0) - 1)
        def _():
            sources = {
                0: [rounded, mid_new.at[pl.ds(0, 8)], mid_new.at[pl.ds(8, 8)], near_new],
                1: [near_new, mid_new.at[pl.ds(0, 8)], mid_new.at[pl.ds(8, 8)], rounded],
            }
            for s in range(4):
                for q in range(4):
                    for c in range(2):

                        @pl.when((lax.rem(place[0] + s, 4) == q) & (core == c))
                        def _():
                            pltpu.make_async_copy(sources[c][q], sends[s], out_sems.at[s]).start()

            for s in range(4):
                pltpu.make_async_copy(rounded, sends[s], out_sems.at[s]).wait()


def rest_kernel(step, last, source_at, idx, place, *refs):
    refs = list(refs)
    take = lambda n: [refs.pop(0) for _ in range(n)]
    blocks = take(2)
    halo, near, mid, far = take(4)
    current = take(2)
    older = take(2) if step else None
    fresh = None if last else take(2)
    rounded = take(2)
    pad, sems = take(2)
    g = pl.program_id(0)
    core = place[1]
    near_at = 24 * (1 - core)
    far_at = 24 * core

    @pl.when(g == 0)
    def _():
        load_all(
            [
                (halo, pad.at[pl.ds(40 * (1 - core), 8)]),
                (near.at[pl.ds(near_at if source_at else 0, 8)], pad.at[pl.ds(8 + near_at, 8)]),
                (mid.at[pl.ds(8 if source_at else 0, 16)], pad.at[pl.ds(16, 16)]),
                (far.at[pl.ds(far_at if source_at else 0, 8)], pad.at[pl.ds(8 + far_at, 8)]),
            ],
            sems,
        )

    for n, first in enumerate((near_at, 8)):
        per = blocks[n].shape[0]
        for r in range(per):
            product = row_product(idx, first + g * per + r, 0, blocks[n], r, pad)
            newer = recurrence(step, product, current[n][r], older[n][r] if step else None)
            if not last:
                fresh[n][r] = newer
            rounded[n][r] = newer.astype(BF)


def filter_call(kernel, name, step, last, source_at, idx, place, parts, moved, halo, rounded, current, older, extra):
    width = halo.shape[-1]
    nnz = parts["blocks"].shape[1]
    blocks = parts["blocks"]
    in_specs, operands, shapes, out_specs = [], [], [], []
    groups = parts["groups"]
    for key, count, per, first in groups:
        in_specs.append(
            pl.BlockSpec((per, nnz, SIZE, SIZE), lambda g, idx, place, per=per, first=first: (g + first(place[1]) // per, 0, 0, 0))
        )
        operands.append(blocks)
    in_specs += [ANY] * (1 + len(moved))
    operands += [halo] + [rounded[key] for key in moved]
    for arrays in [current] + ([older] if step else []):
        at = arrays.get("whole", False)
        for key, count, per, first in groups:
            index = (
                (lambda g, idx, place, per=per, first=first: (g + first(place[1]) // per, 0, 0))
                if at
                else (lambda g, idx, place: (g, 0, 0))
            )
            in_specs.append(pl.BlockSpec((per, SIZE, width), index))
            operands.append(arrays[key])
    scratch = [pltpu.VMEM((parts["window"], SIZE, width), BF), pltpu.SemaphoreType.DMA((1 + len(moved),))]
    for kind in (F32, BF):
        if kind is F32 and last:
            continue
        for key, count, per, first in groups:
            shapes.append(jax.ShapeDtypeStruct((count, SIZE, width), kind))
            out_specs.append(pl.BlockSpec((per, SIZE, width), lambda g, idx, place: (g, 0, 0)))
    if extra:
        in_specs += [ANY] * len(extra)
        operands += extra
        shapes = [jax.ShapeDtypeStruct((8, SIZE, width), BF)] * 4
        out_specs = [ANY] * 4
        scratch += [pltpu.VMEM((8, SIZE, width), BF), pltpu.SemaphoreType.DMA((4,))]
    total = sum(count for _, count, _, _ in groups)
    return pl.pallas_call(
        functools.partial(kernel, step, last, source_at),
        out_shape=shapes,
        grid_spec=pltpu.PrefetchScalarGridSpec(
            num_scalar_prefetch=2,
            grid=(4,),
            in_specs=in_specs,
            out_specs=out_specs,
            scratch_shapes=scratch,
        ),
        compiler_params=params(24),
        cost_estimate=pl.CostEstimate(
            flops=total * nnz * 2 * SIZE * SIZE * width, bytes_accessed=total * MIB // 2, transcendentals=0
        ),
        name=name,
    )(idx, place, *operands)


def chebyshev(vectors, blocks, idx, place):
    rows = lax.axis_size("rows")
    core = place[1]
    within = [(i, i ^ 1) for i in range(rows)]
    between = [(i, i + 1 if i % 2 else i - 1) for i in range(1, rows - 1)]
    far_group = ("far", 8, 2, lambda c: 24 * c)
    near_group = ("near", 8, 2, lambda c: 24 * (1 - c))
    mid_group = ("mid", 16, 4, lambda c: 8)
    far_parts = dict(blocks=blocks, groups=[far_group], window=24)
    rest_parts = dict(blocks=blocks, groups=[near_group, mid_group], window=48)
    start = dict(near=vectors, mid=vectors, far=vectors, whole=True)
    rounded = current = start
    older = None
    far_out = lax.dynamic_slice_in_dim(vectors, 24 * core, 8, 0)
    near_out = lax.dynamic_slice_in_dim(vectors, 24 * (1 - core), 8, 0)
    for step in range(DEGREE):
        last = step == DEGREE - 1
        far_halo = lax.ppermute(far_out, "rows", between)
        near_halo = lax.ppermute(near_out, "rows", within)
        common = (step, last, step == 0, idx, place)
        rest = filter_call(
            rest_kernel, "filter_rest", *common, rest_parts, ["near", "mid", "far"], near_halo, rounded, current, older, None
        )
        extra = rest if last else None
        far = filter_call(
            far_kernel, "filter_far", *common, far_parts, ["far", "mid"], far_halo, rounded, current, older, extra
        )
        if last:
            return far
        older = current
        current = dict(near=rest[0], mid=rest[1], far=far[0])
        rounded = dict(near=rest[2], mid=rest[3], far=far[1])
        near_out, far_out = rounded["near"], rounded["far"]


PAIRS = [(a, b) for a in range(4) for b in range(a, 4)]
HALF = len(PAIRS) // 2


def gram_kernel(total_rows, place, own, got1, got2, got3, keep, send, next1, next2, next3, f, g, sems, out_sems):
    pieces = [own, got1, got2, got3]
    x, core = place[0], place[1]
    load_all([(pieces[s], f.at[lax.rem(x + 4 - s, 4)]) for s in range(4)], sems)
    copies = [
        pltpu.make_async_copy(f.at[lax.rem(x + s + r, 4)], out.at[r - 1], out_sems.at[3 * s + r - 2])
        for s, out in ((1, next1), (2, next2), (3, next3))
        for r in (1, 2, 3)
    ]
    for copy in copies:
        copy.start()
    depth = 8 * SIZE
    width = f.shape[-1]
    for a in range(4):
        left = f[a].reshape(depth, width).T
        for b in range(a, 4):
            n = PAIRS.index((a, b))
            tile = jnp.dot(left, f[b].reshape(depth, width), preferred_element_type=F32)
            g[n // HALF, n % HALF] = tile * (1.0 / total_rows)
    copies.append(pltpu.make_async_copy(g.at[core], keep, out_sems.at[0]))
    copies.append(pltpu.make_async_copy(g.at[1 - core], send, out_sems.at[1]))
    for copy in copies[-2:]:
        copy.start()
    for copy in copies:
        copy.wait()


def gram(total_rows, place, own, got):
    width = own.shape[-1]
    half = jax.ShapeDtypeStruct((HALF, width, width), F32)
    return pl.pallas_call(
        functools.partial(gram_kernel, total_rows),
        out_shape=[half, half] + [jax.ShapeDtypeStruct((3, 8, SIZE, width), BF)] * 3,
        grid_spec=pltpu.PrefetchScalarGridSpec(
            num_scalar_prefetch=1,
            grid=(),
            in_specs=[ANY] * 4,
            out_specs=[ANY] * 5,
            scratch_shapes=[
                pltpu.VMEM((4, 8, SIZE, width), BF),
                pltpu.VMEM((2, HALF, width, width), F32),
                pltpu.SemaphoreType.DMA((4,)),
                pltpu.SemaphoreType.DMA((11,)),
            ],
        ),
        compiler_params=params(24),
        cost_estimate=pl.CostEstimate(flops=10 * 2 * 1024 * 256 * 256, bytes_accessed=8 * MIB, transcendentals=0),
        name="gram",
    )(place, own, *got)


def sum_everywhere(keep, send):
    rows = lax.axis_size("rows")
    vecs = lax.axis_size("vecs")
    swap = [(i, i ^ 1) for i in range(rows)]
    groups = [list(range(c, rows, 2)) for c in range(2)]
    count = rows // 2
    mine = keep + lax.ppermute(send, "rows", swap)
    parts = mine.reshape(count, -1, SIZE)
    parts = lax.all_to_all(parts, "rows", 0, 0, axis_index_groups=groups, tiled=True)
    part = jnp.sum(parts, axis=0)
    others = [lax.ppermute(part, "vecs", [(i, (i + s) % vecs) for i in range(vecs)]) for s in range(1, vecs)]
    part = part + sum(others)
    spread_out = jnp.broadcast_to(part[None], (count,) + part.shape)
    mine = lax.all_to_all(spread_out, "rows", 0, 0, axis_index_groups=groups, tiled=True).reshape(keep.shape)
    return mine, lax.ppermute(mine, "rows", swap), part


def recip(x):
    return pl.reciprocal(x, approx=True)


def inv_sqrt(x):
    y = lax.rsqrt(x)
    return y * (1.5 - 0.5 * x * (y * y))


def spread(x):
    return jnp.broadcast_to(x, (8, SIZE))


def tree_sum(terms):
    while len(terms) > 1:
        terms = [terms[i] + terms[i + 1] if i + 1 < len(terms) else terms[i] for i in range(0, len(terms), 2)]
    return terms[0]


def eliminate(rows):
    count = len(rows)
    lane = lax.broadcasted_iota(jnp.int32, (8, SIZE), 1)
    sub = lax.broadcasted_iota(jnp.int32, (8, SIZE), 0)
    done = []
    for k in range(count):
        base = 8 * k
        inside = (lane >= base) & (lane < base + 8)
        cols = {(q, i): spread(rows[i][:, base + q : base + q + 1]) for i in range(k, count) for q in range(8)}
        s = {(r, q): spread(cols[q, k][r : r + 1, :]) for r in range(8) for q in range(r + 1)}
        own = jnp.where(inside, jnp.where(lane == base + sub, 1.0, 0.0), rows[k])
        row = [spread(own[q : q + 1, :]) for q in range(8)]
        inv = {}
        m = {}
        for j in range(8):
            inv[j] = recip(s[j, j])
            for i in range(j + 1, 8):
                m[i, j] = s[i, j] * inv[j]
            for i in range(j + 1, 8):
                for t in range(j + 1, i + 1):
                    term = (s[i, j] * s[t, j]) * inv[j] if i == t else m[i, j] * s[t, j]
                    s[i, t] = s[i, t] - term
                row[i] = row[i] - m[i, j] * row[j]
        out = None
        for p in range(8):
            scaled = row[p] * inv_sqrt(s[p, p])
            out = scaled if out is None else jnp.where(sub == p, scaled, out)
        done.append(jnp.where(lane <= base + sub, out, 0.0))
        z = [row[p] * inv[p] for p in range(8)]
        for q in range(6, -1, -1):
            for p in range(7, q, -1):
                z[q] = z[q] - m[p, q] * z[p]
        for i in range(k + 1, count):
            rows[i] = jnp.where(inside, 0.0, rows[i]) - tree_sum([cols[q, i] * z[q] for q in range(8)])
    return done


def split3(value):
    high = value.astype(BF)
    rest = value - high.astype(F32)
    mid = rest.astype(BF)
    return high, mid, (rest - mid.astype(F32)).astype(BF)


def factor_kernel(place, mine, other, high_ref, low_ref, w, diag, following, left, right, sems):
    n = 8
    x, core = place[0], place[1]
    at = lambda i: pl.ds(pl.multiple_of(i * SIZE, SIZE), SIZE)
    exact = functools.partial(jnp.dot, preferred_element_type=F32, precision=EXACT)

    def copies(halves):
        return [
            pltpu.make_async_copy(
                halves[m // HALF].at[m % HALF], w.at[pl.ds(256 * a, 256), pl.ds(256 * b, 256)], sems.at[m]
            )
            for m, (a, b) in enumerate(PAIRS)
        ]

    @pl.when(core == 0)
    def _():
        for copy in copies([mine, other]):
            copy.start()

    @pl.when(core == 1)
    def _():
        for copy in copies([other, mine]):
            copy.start()

    diag[...] = jnp.zeros(diag.shape, F32)
    left[...] = jnp.zeros(left.shape, BF)
    for copy in copies([mine, other]):
        copy.wait()
    for a in range(1, 4):
        w[pl.ds(256 * a, 256), pl.ds(0, 256 * a)] = jnp.zeros((256, 256 * a), F32)
    w[pl.ds(n * SIZE, (n - 1) * SIZE), :] = jnp.zeros(((n - 1) * SIZE, n * SIZE), F32)
    following[...] = w[pl.ds(0, SIZE), pl.ds(0, SIZE)]

    def step(k, _):
        done = eliminate([following[pl.ds(8 * r, 8), :] for r in range(16)])
        p = jnp.maximum(k - 1, 0)
        x_prev = diag[...]
        w[at(p), :] = jnp.where(k > 0, exact(x_prev, w[at(p), :]), w[at(p), :])
        w[at(p), at(p)] = jnp.where(k > 0, x_prev, w[at(p), at(p)])
        high, mid, low = split3(jnp.where(k > 0, w[at(p), :], 0.0))
        for t, v in enumerate((high, mid, low, high, mid, high)):
            right[pl.ds(SIZE * t, SIZE), :] = v
        for c in range(n):
            cut = slice(SIZE * c, SIZE * c + SIZE)
            high_t, mid_t, low_t = high[:, cut].T, mid[:, cut].T, low[:, cut].T
            for t, v in enumerate((high_t, high_t, high_t, mid_t, mid_t, low_t)):
                left[pl.ds(SIZE * c, SIZE), pl.ds(SIZE * t, SIZE)] = v
        for t in range(n - 1):
            w[at(k + t), at(p)] = jnp.zeros((SIZE, SIZE), F32)
        for t in range(n - 1):
            w[at(k + t), :] = w[at(k + t), :] - jnp.dot(left[at(k + t), :], right[...], preferred_element_type=F32)
        for r in range(16):
            diag[pl.ds(8 * r, 8), :] = done[r]
        q = jnp.minimum(k + 1, n - 1)
        ahead = exact(diag[...], w[at(k), at(q)])
        following[...] = w[at(q), at(q)] - exact(ahead.T, ahead)
        return 0

    lax.fori_loop(0, n, step, 0)
    end = pl.ds((n - 1) * SIZE, SIZE)
    w[end, :] = exact(diag[...], w[end, :])
    w[end, end] = diag[...]
    for r in range(2):
        row = 2 * x + r
        for c in range(n):
            column = 2 * lax.rem(x + c // 2, 4) + c % 2
            value = jnp.where(column <= row, w[at(row), at(column)], 0.0)
            high = value.astype(BF)
            high_ref[pl.ds(SIZE * r, SIZE), pl.ds(SIZE * c, SIZE)] = high
            low_ref[pl.ds(SIZE * r, SIZE), pl.ds(SIZE * c, SIZE)] = (value - high.astype(F32)).astype(BF)


def factor(place, mine, other):
    n = 8
    vmem = pl.BlockSpec(memory_space=pltpu.VMEM)
    return pl.pallas_call(
        factor_kernel,
        out_shape=[jax.ShapeDtypeStruct((2 * SIZE, n * SIZE), BF)] * 2,
        grid_spec=pltpu.PrefetchScalarGridSpec(
            num_scalar_prefetch=1,
            grid=(),
            in_specs=[ANY] * 2,
            out_specs=[vmem] * 2,
            scratch_shapes=[
                pltpu.VMEM(((2 * n - 1) * SIZE, n * SIZE), F32),
                pltpu.VMEM((SIZE, SIZE), F32),
                pltpu.VMEM((SIZE, SIZE), F32),
                pltpu.VMEM(((2 * n - 1) * SIZE, 6 * SIZE), BF),
                pltpu.VMEM((6 * SIZE, n * SIZE), BF),
                pltpu.SemaphoreType.DMA((len(PAIRS),)),
            ],
        ),
        compiler_params=params(32),
        cost_estimate=pl.CostEstimate(flops=20_000_000_000, bytes_accessed=4 * MIB, transcendentals=0),
        name="factor",
    )(place, mine, other)


def apply_kernel(place, *refs):
    own, got, far = refs[0:4], refs[4:7], refs[7:10]
    high, low, out, tiles, sems = refs[10:]
    x = place[0]
    t = pl.program_id(0)
    steps = pl.num_programs(0)
    per = own[0].shape[0]
    width = own[0].shape[-1]
    dims = (((1,), (1,)), ((), ()))
    slot = lax.rem(t, 2)

    def copies(slot, t):
        return [
            pltpu.make_async_copy(
                tiles.at[slot, s], out.at[lax.rem(x + 4 - s, 4), pl.ds(t * per, per)], sems.at[slot, s]
            )
            for s in range(4)
        ]

    @pl.when(t >= 2)
    def _():
        for copy in copies(slot, t - 2):
            copy.wait()

    for s in range(4):
        if s == 0:
            panels = [own[0][...], got[2][...], got[1][...], got[0][...]]
        else:
            panels = [own[4 - s][...]] + [far[s - 1][r] for r in range(3)]
        left = jnp.concatenate([p.reshape(per * SIZE, width) for p in panels], axis=1)
        value = lax.dot_general(left, high[...], dims, preferred_element_type=F32)
        value = value + lax.dot_general(left, low[...], dims, preferred_element_type=F32)
        tiles[slot, s] = value.reshape(per, SIZE, width)
    for copy in copies(slot, t):
        copy.start()

    @pl.when(t == steps - 1)
    def _():
        for copy in copies(1 - slot, t - 1) + copies(slot, t):
            copy.wait()


def apply(place, own, got, far, high, low):
    width = own[0].shape[-1]
    per = 2
    whole = pl.BlockSpec(high.shape, lambda t, *_: (0, 0))
    rows = pl.BlockSpec((per, SIZE, width), lambda t, *_: (t, 0, 0))
    return pl.pallas_call(
        apply_kernel,
        out_shape=jax.ShapeDtypeStruct((4, 8, SIZE, width), F32),
        grid_spec=pltpu.PrefetchScalarGridSpec(
            num_scalar_prefetch=1,
            grid=(8 // per,),
            in_specs=[rows] * 7 + [pl.BlockSpec((3, per, SIZE, width), lambda t, *_: (0, t, 0, 0))] * 3 + [whole, whole],
            out_specs=ANY,
            scratch_shapes=[pltpu.VMEM((2, 4, per, SIZE, width), F32), pltpu.SemaphoreType.DMA((2, 4))],
        ),
        compiler_params=params(32),
        cost_estimate=pl.CostEstimate(flops=4 * 1024 * 1024 * 256 * 4, bytes_accessed=14 * MIB, transcendentals=0),
        name="apply",
    )(place, *own, *got, *far, high, low)


def shards(vectors, blocks, columns):
    block_rows = blocks.shape[0]
    width = vectors.shape[1]
    row = lax.axis_index("rows")
    x = lax.axis_index("vecs")
    vecs = lax.axis_size("vecs")
    total_rows = vectors.shape[0] * lax.axis_size("rows")
    idx = columns - row * block_rows + REACH
    place = jnp.stack([x, lax.rem(row, 2)]).astype(jnp.int32)
    own = chebyshev(vectors.reshape(block_rows, SIZE, width), blocks, idx, place)
    shift = lambda a, s: lax.ppermute(a, "vecs", [(i, (i + s) % vecs) for i in range(vecs)])
    got = [shift(own[s], s) for s in range(1, vecs)]
    keep, send, *following = gram(total_rows, place, own[0], got)
    mine, other, part = sum_everywhere(keep, send)
    far = [shift(following[s - 1], s) for s in range(1, vecs)]
    inverse_high, inverse_low = factor(place, mine, other)
    return apply(place, own, got, far, inverse_high, inverse_low).reshape(vectors.shape)


def solution(mesh):
    in_specs = (P("rows", "vecs"), P("rows", None, None, None), P("rows", None))
    out_specs = P("rows", "vecs")
    return jax.shard_map(shards, mesh=mesh, in_specs=in_specs, out_specs=out_specs, check_vma=False)
```

```python
import functools

import jax
import jax.numpy as jnp
from jax import lax
from jax.experimental import pallas as pl
from jax.experimental.pallas import tpu as pltpu
from jax.sharding import PartitionSpec as P

DEGREE = 4
filter_center = 0.25
filter_radius = 1.25

F32 = jnp.float32
BF = jnp.bfloat16
EXACT = lax.Precision.HIGHEST
SIZE = 128
REACH = 8
MIB = 1 << 20

ANY = pl.BlockSpec(memory_space=pl.ANY)


def params(mib):
    return pltpu.CompilerParams(vmem_limit_bytes=mib * MIB)


def load_all(pairs, sems):
    copies = [pltpu.make_async_copy(src, dst, sems.at[n]) for n, (src, dst) in enumerate(pairs)]
    for copy in copies:
        copy.start()
    for copy in copies:
        copy.wait()


def row_product(idx, row, shift, blocks_ref, r, pad):
    count = blocks_ref.shape[1]
    left = jnp.concatenate([blocks_ref[r, j] for j in range(count)], axis=1)
    right = jnp.concatenate([pad[idx[row, j] - shift] for j in range(count)], axis=0)
    return jnp.dot(left, right, preferred_element_type=F32)


def recurrence(step, product, current, older):
    scale = (2.0 if step else 1.0) / filter_radius
    newer = scale * product - (scale * filter_center) * current.astype(F32)
    return newer - older.astype(F32) if step else newer


def far_kernel(step, last, source_at, idx, place, *refs):
    refs = list(refs)
    take = lambda n: [refs.pop(0) for _ in range(n)]
    (blocks,) = take(1)
    halo, far, mid = take(3)
    (current,) = take(1)
    older = take(1)[0] if step else None
    if last:
        near_new, mid_new = take(2)
        sends = take(4)
        pad, sems, rounded, out_sems = take(4)
    else:
        fresh, rounded = take(2)
        pad, sems = take(2)
    g = pl.program_id(0)
    per = blocks.shape[0]
    core = place[1]
    far_at = 24 * core if source_at else 0
    mid_at = 8 if source_at else 0

    @pl.when(g == 0)
    def _():
        load_all(
            [
                (halo, pad.at[pl.ds(16 * core, 8)]),
                (far.at[pl.ds(far_at, 8)], pad.at[pl.ds(8, 8)]),
                (mid.at[pl.ds(mid_at + 8 * core, 8)], pad.at[pl.ds(16 * (1 - core), 8)]),
            ],
            sems,
        )

    for r in range(per):
        product = row_product(idx, 24 * core + g * per + r, 24 * core, blocks, r, pad)
        newer = recurrence(step, product, current[r], older[r] if step else None)
        if last:
            rounded[g * per + r] = newer.astype(BF)
        else:
            fresh[r] = newer
            rounded[r] = newer.astype(BF)

    if last:

        @pl.when(g == pl.num_programs(0) - 1)
        def _():
            sources = {
                0: [rounded, mid_new.at[pl.ds(0, 8)], mid_new.at[pl.ds(8, 8)], near_new],
                1: [near_new, mid_new.at[pl.ds(0, 8)], mid_new.at[pl.ds(8, 8)], rounded],
            }
            for s in range(4):
                for q in range(4):
                    for c in range(2):

                        @pl.when((lax.rem(place[0] + s, 4) == q) & (core == c))
                        def _():
                            pltpu.make_async_copy(sources[c][q], sends[s], out_sems.at[s]).start()

            for s in range(4):
                pltpu.make_async_copy(rounded, sends[s], out_sems.at[s]).wait()


def rest_kernel(step, last, source_at, idx, place, *refs):
    refs = list(refs)
    take = lambda n: [refs.pop(0) for _ in range(n)]
    blocks = take(2)
    halo, near, mid, far = take(4)
    current = take(2)
    older = take(2) if step else None
    fresh = None if last else take(2)
    rounded = take(2)
    pad, sems = take(2)
    g = pl.program_id(0)
    core = place[1]
    near_at = 24 * (1 - core)
    far_at = 24 * core

    @pl.when(g == 0)
    def _():
        load_all(
            [
                (halo, pad.at[pl.ds(40 * (1 - core), 8)]),
                (near.at[pl.ds(near_at if source_at else 0, 8)], pad.at[pl.ds(8 + near_at, 8)]),
                (mid.at[pl.ds(8 if source_at else 0, 16)], pad.at[pl.ds(16, 16)]),
                (far.at[pl.ds(far_at if source_at else 0, 8)], pad.at[pl.ds(8 + far_at, 8)]),
            ],
            sems,
        )

    for n, first in enumerate((near_at, 8)):
        per = blocks[n].shape[0]
        for r in range(per):
            product = row_product(idx, first + g * per + r, 0, blocks[n], r, pad)
            newer = recurrence(step, product, current[n][r], older[n][r] if step else None)
            if not last:
                fresh[n][r] = newer
            rounded[n][r] = newer.astype(BF)


def filter_call(kernel, name, step, last, source_at, idx, place, parts, moved, halo, rounded, current, older, extra):
    width = halo.shape[-1]
    nnz = parts["blocks"].shape[1]
    blocks = parts["blocks"]
    in_specs, operands, shapes, out_specs = [], [], [], []
    groups = parts["groups"]
    for key, count, per, first in groups:
        in_specs.append(
            pl.BlockSpec((per, nnz, SIZE, SIZE), lambda g, idx, place, per=per, first=first: (g + first(place[1]) // per, 0, 0, 0))
        )
        operands.append(blocks)
    in_specs += [ANY] * (1 + len(moved))
    operands += [halo] + [rounded[key] for key in moved]
    for arrays in [current] + ([older] if step else []):
        at = arrays.get("whole", False)
        for key, count, per, first in groups:
            index = (
                (lambda g, idx, place, per=per, first=first: (g + first(place[1]) // per, 0, 0))
                if at
                else (lambda g, idx, place: (g, 0, 0))
            )
            in_specs.append(pl.BlockSpec((per, SIZE, width), index))
            operands.append(arrays[key])
    scratch = [pltpu.VMEM((parts["window"], SIZE, width), BF), pltpu.SemaphoreType.DMA((1 + len(moved),))]
    for kind in (F32, BF):
        if kind is F32 and last:
            continue
        for key, count, per, first in groups:
            shapes.append(jax.ShapeDtypeStruct((count, SIZE, width), kind))
            out_specs.append(pl.BlockSpec((per, SIZE, width), lambda g, idx, place: (g, 0, 0)))
    if extra:
        in_specs += [ANY] * len(extra)
        operands += extra
        shapes = [jax.ShapeDtypeStruct((8, SIZE, width), BF)] * 4
        out_specs = [ANY] * 4
        scratch += [pltpu.VMEM((8, SIZE, width), BF), pltpu.SemaphoreType.DMA((4,))]
    total = sum(count for _, count, _, _ in groups)
    return pl.pallas_call(
        functools.partial(kernel, step, last, source_at),
        out_shape=shapes,
        grid_spec=pltpu.PrefetchScalarGridSpec(
            num_scalar_prefetch=2,
            grid=(4,),
            in_specs=in_specs,
            out_specs=out_specs,
            scratch_shapes=scratch,
        ),
        compiler_params=params(24),
        cost_estimate=pl.CostEstimate(
            flops=total * nnz * 2 * SIZE * SIZE * width, bytes_accessed=total * MIB // 2, transcendentals=0
        ),
        name=name,
    )(idx, place, *operands)


def chebyshev(vectors, blocks, idx, place):
    rows = lax.axis_size("rows")
    core = place[1]
    within = [(i, i ^ 1) for i in range(rows)]
    between = [(i, i + 1 if i % 2 else i - 1) for i in range(1, rows - 1)]
    far_group = ("far", 8, 2, lambda c: 24 * c)
    near_group = ("near", 8, 2, lambda c: 24 * (1 - c))
    mid_group = ("mid", 16, 4, lambda c: 8)
    far_parts = dict(blocks=blocks, groups=[far_group], window=24)
    rest_parts = dict(blocks=blocks, groups=[near_group, mid_group], window=48)
    start = dict(near=vectors, mid=vectors, far=vectors, whole=True)
    rounded = current = start
    older = None
    far_out = lax.dynamic_slice_in_dim(vectors, 24 * core, 8, 0)
    near_out = lax.dynamic_slice_in_dim(vectors, 24 * (1 - core), 8, 0)
    for step in range(DEGREE):
        last = step == DEGREE - 1
        far_halo = lax.ppermute(far_out, "rows", between)
        near_halo = lax.ppermute(near_out, "rows", within)
        common = (step, last, step == 0, idx, place)
        rest = filter_call(
            rest_kernel, "filter_rest", *common, rest_parts, ["near", "mid", "far"], near_halo, rounded, current, older, None
        )
        extra = rest if last else None
        far = filter_call(
            far_kernel, "filter_far", *common, far_parts, ["far", "mid"], far_halo, rounded, current, older, extra
        )
        if last:
            return far
        older = current
        current = dict(near=rest[0], mid=rest[1], far=far[0])
        rounded = dict(near=rest[2], mid=rest[3], far=far[1])
        near_out, far_out = rounded["near"], rounded["far"]


PAIRS = [(a, b) for a in range(4) for b in range(a, 4)]
HALF = len(PAIRS) // 2


def gram_kernel(total_rows, place, own, got1, got2, got3, keep, send, next1, next2, next3, f, g, sems, out_sems):
    pieces = [own, got1, got2, got3]
    x, core = place[0], place[1]
    load_all([(pieces[s], f.at[lax.rem(x + 4 - s, 4)]) for s in range(4)], sems)
    copies = [
        pltpu.make_async_copy(f.at[lax.rem(x + s + r, 4)], out.at[r - 1], out_sems.at[3 * s + r - 2])
        for s, out in ((1, next1), (2, next2), (3, next3))
        for r in (1, 2, 3)
    ]
    for copy in copies:
        copy.start()
    depth = 8 * SIZE
    width = f.shape[-1]
    for a in range(4):
        left = f[a].reshape(depth, width).T
        for b in range(a, 4):
            n = PAIRS.index((a, b))
            tile = jnp.dot(left, f[b].reshape(depth, width), preferred_element_type=F32)
            g[n // HALF, n % HALF] = tile * (1.0 / total_rows)
    copies.append(pltpu.make_async_copy(g.at[core], keep, out_sems.at[0]))
    copies.append(pltpu.make_async_copy(g.at[1 - core], send, out_sems.at[1]))
    for copy in copies[-2:]:
        copy.start()
    for copy in copies:
        copy.wait()


def gram(total_rows, place, own, got):
    width = own.shape[-1]
    half = jax.ShapeDtypeStruct((HALF, width, width), F32)
    return pl.pallas_call(
        functools.partial(gram_kernel, total_rows),
        out_shape=[half, half] + [jax.ShapeDtypeStruct((3, 8, SIZE, width), BF)] * 3,
        grid_spec=pltpu.PrefetchScalarGridSpec(
            num_scalar_prefetch=1,
            grid=(),
            in_specs=[ANY] * 4,
            out_specs=[ANY] * 5,
            scratch_shapes=[
                pltpu.VMEM((4, 8, SIZE, width), BF),
                pltpu.VMEM((2, HALF, width, width), F32),
                pltpu.SemaphoreType.DMA((4,)),
                pltpu.SemaphoreType.DMA((11,)),
            ],
        ),
        compiler_params=params(24),
        cost_estimate=pl.CostEstimate(flops=10 * 2 * 1024 * 256 * 256, bytes_accessed=8 * MIB, transcendentals=0),
        name="gram",
    )(place, own, *got)


def sum_everywhere(keep, send):
    rows = lax.axis_size("rows")
    vecs = lax.axis_size("vecs")
    swap = [(i, i ^ 1) for i in range(rows)]
    groups = [list(range(c, rows, 2)) for c in range(2)]
    count = rows // 2
    mine = keep + lax.ppermute(send, "rows", swap)
    parts = mine.reshape(count, -1, mine.shape[-1])
    parts = lax.all_to_all(parts, "rows", 0, 0, axis_index_groups=groups, tiled=True)
    part = jnp.sum(parts, axis=0)
    others = [lax.ppermute(part, "vecs", [(i, (i + s) % vecs) for i in range(vecs)]) for s in range(1, vecs)]
    part = part + sum(others)
    spread_out = jnp.broadcast_to(part[None], (count,) + part.shape)
    mine = lax.all_to_all(spread_out, "rows", 0, 0, axis_index_groups=groups, tiled=True).reshape(keep.shape)
    return mine, lax.ppermute(mine, "rows", swap), part


def recip(x):
    return pl.reciprocal(x, approx=True)


def inv_sqrt(x):
    y = lax.rsqrt(x)
    return y * (1.5 - 0.5 * x * (y * y))


def spread(x):
    return jnp.broadcast_to(x, (8, SIZE))


def tree_sum(terms):
    while len(terms) > 1:
        terms = [terms[i] + terms[i + 1] if i + 1 < len(terms) else terms[i] for i in range(0, len(terms), 2)]
    return terms[0]


def eliminate(rows):
    count = len(rows)
    lane = lax.broadcasted_iota(jnp.int32, (8, SIZE), 1)
    sub = lax.broadcasted_iota(jnp.int32, (8, SIZE), 0)
    done = []
    for k in range(count):
        base = 8 * k
        inside = (lane >= base) & (lane < base + 8)
        cols = {(q, i): spread(rows[i][:, base + q : base + q + 1]) for i in range(k, count) for q in range(8)}
        s = {(r, q): spread(cols[q, k][r : r + 1, :]) for r in range(8) for q in range(r + 1)}
        own = jnp.where(inside, jnp.where(lane == base + sub, 1.0, 0.0), rows[k])
        row = [spread(own[q : q + 1, :]) for q in range(8)]
        inv = {}
        m = {}
        for j in range(8):
            inv[j] = recip(s[j, j])
            for i in range(j + 1, 8):
                m[i, j] = s[i, j] * inv[j]
            for i in range(j + 1, 8):
                for t in range(j + 1, i + 1):
                    term = (s[i, j] * s[t, j]) * inv[j] if i == t else m[i, j] * s[t, j]
                    s[i, t] = s[i, t] - term
                row[i] = row[i] - m[i, j] * row[j]
        out = None
        for p in range(8):
            scaled = row[p] * inv_sqrt(s[p, p])
            out = scaled if out is None else jnp.where(sub == p, scaled, out)
        done.append(jnp.where(lane <= base + sub, out, 0.0))
        z = [row[p] * inv[p] for p in range(8)]
        for q in range(6, -1, -1):
            for p in range(7, q, -1):
                z[q] = z[q] - m[p, q] * z[p]
        for i in range(k + 1, count):
            rows[i] = jnp.where(inside, 0.0, rows[i]) - tree_sum([cols[q, i] * z[q] for q in range(8)])
    return done


def split3(value):
    high = value.astype(BF)
    rest = value - high.astype(F32)
    mid = rest.astype(BF)
    return high, mid, (rest - mid.astype(F32)).astype(BF)


def factor_kernel(place, mine, other, high_ref, low_ref, w, diag, following, left, right, sems):
    n = 8
    x, core = place[0], place[1]
    at = lambda i: pl.ds(pl.multiple_of(i * SIZE, SIZE), SIZE)
    exact = functools.partial(jnp.dot, preferred_element_type=F32, precision=EXACT)

    def copies(halves):
        return [
            pltpu.make_async_copy(
                halves[m // HALF].at[m % HALF], w.at[pl.ds(256 * a, 256), pl.ds(256 * b, 256)], sems.at[m]
            )
            for m, (a, b) in enumerate(PAIRS)
        ]

    @pl.when(core == 0)
    def _():
        for copy in copies([mine, other]):
            copy.start()

    @pl.when(core == 1)
    def _():
        for copy in copies([other, mine]):
            copy.start()

    diag[...] = jnp.zeros(diag.shape, F32)
    left[...] = jnp.zeros(left.shape, BF)
    for copy in copies([mine, other]):
        copy.wait()
    for a in range(1, 4):
        w[pl.ds(256 * a, 256), pl.ds(0, 256 * a)] = jnp.zeros((256, 256 * a), F32)
    w[pl.ds(n * SIZE, (n - 1) * SIZE), :] = jnp.zeros(((n - 1) * SIZE, n * SIZE), F32)
    following[...] = w[pl.ds(0, SIZE), pl.ds(0, SIZE)]

    def step(k, _):
        done = eliminate([following[pl.ds(8 * r, 8), :] for r in range(16)])
        p = jnp.maximum(k - 1, 0)
        x_prev = diag[...]
        w[at(p), :] = jnp.where(k > 0, exact(x_prev, w[at(p), :]), w[at(p), :])
        w[at(p), at(p)] = jnp.where(k > 0, x_prev, w[at(p), at(p)])
        high, mid, low = split3(jnp.where(k > 0, w[at(p), :], 0.0))
        for t, v in enumerate((high, mid, low, high, mid, high)):
            right[pl.ds(SIZE * t, SIZE), :] = v
        for c in range(n):
            cut = slice(SIZE * c, SIZE * c + SIZE)
            high_t, mid_t, low_t = high[:, cut].T, mid[:, cut].T, low[:, cut].T
            for t, v in enumerate((high_t, high_t, high_t, mid_t, mid_t, low_t)):
                left[pl.ds(SIZE * c, SIZE), pl.ds(SIZE * t, SIZE)] = v
        for t in range(n - 1):
            w[at(k + t), at(p)] = jnp.zeros((SIZE, SIZE), F32)
        for t in range(n - 1):
            w[at(k + t), :] = w[at(k + t), :] - jnp.dot(left[at(k + t), :], right[...], preferred_element_type=F32)
        for r in range(16):
            diag[pl.ds(8 * r, 8), :] = done[r]
        q = jnp.minimum(k + 1, n - 1)
        ahead = exact(diag[...], w[at(k), at(q)])
        following[...] = w[at(q), at(q)] - exact(ahead.T, ahead)
        return 0

    lax.fori_loop(0, n, step, 0)
    end = pl.ds((n - 1) * SIZE, SIZE)
    w[end, :] = exact(diag[...], w[end, :])
    w[end, end] = diag[...]
    for r in range(2):
        row = 2 * x + r
        for c in range(n):
            column = 2 * lax.rem(x + c // 2, 4) + c % 2
            value = jnp.where(column <= row, w[at(row), at(column)], 0.0)
            value = value.T
            high = value.astype(BF)
            high_ref[pl.ds(SIZE * c, SIZE), pl.ds(SIZE * r, SIZE)] = high
            low_ref[pl.ds(SIZE * c, SIZE), pl.ds(SIZE * r, SIZE)] = (value - high.astype(F32)).astype(BF)


def factor(place, mine, other):
    n = 8
    vmem = pl.BlockSpec(memory_space=pltpu.VMEM)
    return pl.pallas_call(
        factor_kernel,
        out_shape=[jax.ShapeDtypeStruct((n * SIZE, 2 * SIZE), BF)] * 2,
        grid_spec=pltpu.PrefetchScalarGridSpec(
            num_scalar_prefetch=1,
            grid=(),
            in_specs=[ANY] * 2,
            out_specs=[vmem] * 2,
            scratch_shapes=[
                pltpu.VMEM(((2 * n - 1) * SIZE, n * SIZE), F32),
                pltpu.VMEM((SIZE, SIZE), F32),
                pltpu.VMEM((SIZE, SIZE), F32),
                pltpu.VMEM(((2 * n - 1) * SIZE, 6 * SIZE), BF),
                pltpu.VMEM((6 * SIZE, n * SIZE), BF),
                pltpu.SemaphoreType.DMA((len(PAIRS),)),
            ],
        ),
        compiler_params=params(32),
        cost_estimate=pl.CostEstimate(flops=1_000_000, bytes_accessed=4 * MIB, transcendentals=0),
        name="factor",
    )(place, mine, other)


def apply_kernel(place, *refs):
    own, got, far = refs[0:4], refs[4:7], refs[7:10]
    high, low, out, tiles, sems = refs[10:]
    x = place[0]
    t = pl.program_id(0)
    steps = pl.num_programs(0)
    per = own[0].shape[0]
    width = own[0].shape[-1]
    slot = lax.rem(t, 2)

    def copies(slot, t):
        return [
            pltpu.make_async_copy(
                tiles.at[slot, s], out.at[lax.rem(x + 4 - s, 4), pl.ds(t * per, per)], sems.at[slot, s]
            )
            for s in range(4)
        ]

    @pl.when(t >= 2)
    def _():
        for copy in copies(slot, t - 2):
            copy.wait()

    for s in range(4):
        if s == 0:
            panels = [own[0][...], got[2][...], got[1][...], got[0][...]]
        else:
            panels = [own[4 - s][...]] + [far[s - 1][r] for r in range(3)]
        left = jnp.concatenate([p.reshape(per * SIZE, width) for p in panels], axis=1)
        value = jnp.dot(left, high[...], preferred_element_type=F32)
        value = value + jnp.dot(left, low[...], preferred_element_type=F32)
        tiles[slot, s] = value.reshape(per, SIZE, width)
    for copy in copies(slot, t):
        copy.start()

    @pl.when(t == steps - 1)
    def _():
        for copy in copies(1 - slot, t - 1) + copies(slot, t):
            copy.wait()


def apply(place, own, got, far, high, low):
    width = own[0].shape[-1]
    per = 2
    whole = pl.BlockSpec(high.shape, lambda t, *_: (0, 0))
    rows = pl.BlockSpec((per, SIZE, width), lambda t, *_: (t, 0, 0))
    return pl.pallas_call(
        apply_kernel,
        out_shape=jax.ShapeDtypeStruct((4, 8, SIZE, width), F32),
        grid_spec=pltpu.PrefetchScalarGridSpec(
            num_scalar_prefetch=1,
            grid=(8 // per,),
            in_specs=[rows] * 7 + [pl.BlockSpec((3, per, SIZE, width), lambda t, *_: (0, t, 0, 0))] * 3 + [whole, whole],
            out_specs=ANY,
            scratch_shapes=[pltpu.VMEM((2, 4, per, SIZE, width), F32), pltpu.SemaphoreType.DMA((2, 4))],
        ),
        compiler_params=params(32),
        cost_estimate=pl.CostEstimate(flops=4 * 1024 * 1024 * 256 * 4, bytes_accessed=14 * MIB, transcendentals=0),
        name="apply",
    )(place, *own, *got, *far, high, low)


def shards(vectors, blocks, columns):
    block_rows = blocks.shape[0]
    width = vectors.shape[1]
    row = lax.axis_index("rows")
    x = lax.axis_index("vecs")
    vecs = lax.axis_size("vecs")
    total_rows = vectors.shape[0] * lax.axis_size("rows")
    idx = columns - row * block_rows + REACH
    place = jnp.stack([x, lax.rem(row, 2)]).astype(jnp.int32)
    own = chebyshev(vectors.reshape(block_rows, SIZE, width), blocks, idx, place)
    shift = lambda a, s: lax.ppermute(a, "vecs", [(i, (i + s) % vecs) for i in range(vecs)])
    got = [shift(own[s], s) for s in range(1, vecs)]
    keep, send, *following = gram(total_rows, place, own[0], got)
    mine, other, part = sum_everywhere(keep, send)
    far = [shift(following[s - 1], s) for s in range(1, vecs)]
    inverse_high, inverse_low = factor(place, mine, other)
    return apply(place, own, got, far, inverse_high, inverse_low).reshape(vectors.shape)


def solution(mesh):
    in_specs = (P("rows", "vecs"), P("rows", None, None, None), P("rows", None))
    out_specs = P("rows", "vecs")
    return jax.shard_map(shards, mesh=mesh, in_specs=in_specs, out_specs=out_specs, check_vma=False)
```

```python
import functools

import jax
import jax.numpy as jnp
from jax import lax
from jax.experimental import pallas as pl
from jax.experimental.pallas import tpu as pltpu
from jax.sharding import PartitionSpec as P

DEGREE = 4
filter_center = 0.25
filter_radius = 1.25

F32 = jnp.float32
BF = jnp.bfloat16
EXACT = lax.Precision.HIGHEST
SIZE = 128
REACH = 8
MIB = 1 << 20

ANY = pl.BlockSpec(memory_space=pl.ANY)


def params(mib):
    return pltpu.CompilerParams(vmem_limit_bytes=mib * MIB)


def load_all(pairs, sems):
    copies = [pltpu.make_async_copy(src, dst, sems.at[n]) for n, (src, dst) in enumerate(pairs)]
    for copy in copies:
        copy.start()
    for copy in copies:
        copy.wait()


def row_product(idx, row, shift, blocks_ref, r, pad):
    count = blocks_ref.shape[1]
    left = jnp.concatenate([blocks_ref[r, j] for j in range(count)], axis=1)
    right = jnp.concatenate([pad[idx[row, j] - shift] for j in range(count)], axis=0)
    return jnp.dot(left, right, preferred_element_type=F32)


def recurrence(step, product, current, older):
    scale = (2.0 if step else 1.0) / filter_radius
    newer = scale * product - (scale * filter_center) * current.astype(F32)
    return newer - older.astype(F32) if step else newer


def far_kernel(step, last, source_at, idx, place, *refs):
    refs = list(refs)
    take = lambda n: [refs.pop(0) for _ in range(n)]
    (blocks,) = take(1)
    halo, far, mid = take(3)
    (current,) = take(1)
    older = take(1)[0] if step else None
    fresh = None if last else take(1)[0]
    rounded, pad, sems = take(3)
    g = pl.program_id(0)
    per = blocks.shape[0]
    core = place[1]
    far_at = 24 * core if source_at else 0
    mid_at = 8 if source_at else 0

    @pl.when(g == 0)
    def _():
        load_all(
            [
                (halo, pad.at[pl.ds(16 * core, 8)]),
                (far.at[pl.ds(far_at, 8)], pad.at[pl.ds(8, 8)]),
                (mid.at[pl.ds(mid_at + 8 * core, 8)], pad.at[pl.ds(16 * (1 - core), 8)]),
            ],
            sems,
        )

    for r in range(per):
        product = row_product(idx, 24 * core + g * per + r, 24 * core, blocks, r, pad)
        newer = recurrence(step, product, current[r], older[r] if step else None)
        if not last:
            fresh[r] = newer
        rounded[r] = newer.astype(BF)


def rest_kernel(step, last, source_at, idx, place, *refs):
    refs = list(refs)
    take = lambda n: [refs.pop(0) for _ in range(n)]
    blocks = take(2)
    halo, near, mid, far = take(4)
    current = take(2)
    older = take(2) if step else None
    if last:
        sends = take(4)
        pad, sems, near_new, mid_new, out_sems = take(5)
        rounded = [near_new, mid_new]
    else:
        fresh = take(2)
        rounded = take(2)
        pad, sems = take(2)
    g = pl.program_id(0)
    core = place[1]
    near_at = 24 * (1 - core)
    far_at = 24 * core

    @pl.when(g == 0)
    def _():
        load_all(
            [
                (halo, pad.at[pl.ds(40 * (1 - core), 8)]),
                (near.at[pl.ds(near_at if source_at else 0, 8)], pad.at[pl.ds(8 + near_at, 8)]),
                (mid.at[pl.ds(8 if source_at else 0, 16)], pad.at[pl.ds(16, 16)]),
                (far.at[pl.ds(far_at if source_at else 0, 8)], pad.at[pl.ds(8 + far_at, 8)]),
            ],
            sems,
        )

    for n, first in enumerate((near_at, 8)):
        per = blocks[n].shape[0]
        for r in range(per):
            product = row_product(idx, first + g * per + r, 0, blocks[n], r, pad)
            newer = recurrence(step, product, current[n][r], older[n][r] if step else None)
            if last:
                rounded[n][g * per + r] = newer.astype(BF)
            else:
                fresh[n][r] = newer
                rounded[n][r] = newer.astype(BF)

    if last:

        @pl.when(g == pl.num_programs(0) - 1)
        def _():
            halves = [mid_new.at[pl.ds(0, 8)], mid_new.at[pl.ds(8, 8)]]
            sources = {0: [near_new, halves[0], halves[1], near_new], 1: [near_new, halves[1], halves[0], near_new]}
            for s in range(4):
                for q in range(4):
                    for c in range(2):

                        @pl.when((lax.rem(place[2] + s, 4) == q) & (core == c))
                        def _():
                            pltpu.make_async_copy(sources[c][q], sends[s], out_sems.at[s]).start()

            for s in range(4):
                pltpu.make_async_copy(near_new, sends[s], out_sems.at[s]).wait()


def filter_call(kernel, name, step, last, source_at, idx, place, parts, moved, halo, rounded, current, older, route):
    width = halo.shape[-1]
    nnz = parts["blocks"].shape[1]
    blocks = parts["blocks"]
    in_specs, operands, shapes, out_specs = [], [], [], []
    groups = parts["groups"]
    for key, count, per, first in groups:
        in_specs.append(
            pl.BlockSpec((per, nnz, SIZE, SIZE), lambda g, idx, place, per=per, first=first: (g + first(place[1]) // per, 0, 0, 0))
        )
        operands.append(blocks)
    in_specs += [ANY] * (1 + len(moved))
    operands += [halo] + [rounded[key] for key in moved]
    for arrays in [current] + ([older] if step else []):
        at = arrays.get("whole", False)
        for key, count, per, first in groups:
            index = (
                (lambda g, idx, place, per=per, first=first: (g + first(place[1]) // per, 0, 0))
                if at
                else (lambda g, idx, place: (g, 0, 0))
            )
            in_specs.append(pl.BlockSpec((per, SIZE, width), index))
            operands.append(arrays[key])
    scratch = [pltpu.VMEM((parts["window"], SIZE, width), BF), pltpu.SemaphoreType.DMA((1 + len(moved),))]
    for kind in (F32, BF):
        if kind is F32 and last:
            continue
        for key, count, per, first in groups:
            shapes.append(jax.ShapeDtypeStruct((count, SIZE, width), kind))
            out_specs.append(pl.BlockSpec((per, SIZE, width), lambda g, idx, place: (g, 0, 0)))
    if route:
        shapes = [jax.ShapeDtypeStruct((8, SIZE, width), BF)] * 4
        out_specs = [ANY] * 4
        scratch += [pltpu.VMEM((count, SIZE, width), BF) for _, count, _, _ in groups] + [pltpu.SemaphoreType.DMA((4,))]
    total = sum(count for _, count, _, _ in groups)
    return pl.pallas_call(
        functools.partial(kernel, step, last, source_at),
        out_shape=shapes,
        grid_spec=pltpu.PrefetchScalarGridSpec(
            num_scalar_prefetch=2,
            grid=(4,),
            in_specs=in_specs,
            out_specs=out_specs,
            scratch_shapes=scratch,
        ),
        compiler_params=params(24),
        cost_estimate=pl.CostEstimate(
            flops=total * nnz * 2 * SIZE * SIZE * width, bytes_accessed=total * MIB // 2, transcendentals=0
        ),
        name=name,
    )(idx, place, *operands)


def chebyshev(vectors, blocks, idx, place):
    rows = lax.axis_size("rows")
    core = place[1]
    within = [(i, i ^ 1) for i in range(rows)]
    between = [(i, i + 1 if i % 2 else i - 1) for i in range(1, rows - 1)]
    far_group = ("far", 8, 2, lambda c: 24 * c)
    near_group = ("near", 8, 2, lambda c: 24 * (1 - c))
    mid_group = ("mid", 16, 4, lambda c: 8)
    far_parts = dict(blocks=blocks, groups=[far_group], window=24)
    rest_parts = dict(blocks=blocks, groups=[near_group, mid_group], window=48)
    start = dict(near=vectors, mid=vectors, far=vectors, whole=True)
    rounded = current = start
    older = None
    far_out = lax.dynamic_slice_in_dim(vectors, 24 * core, 8, 0)
    near_out = lax.dynamic_slice_in_dim(vectors, 24 * (1 - core), 8, 0)
    for step in range(DEGREE):
        last = step == DEGREE - 1
        far_halo = lax.ppermute(far_out, "rows", between)
        near_halo = lax.ppermute(near_out, "rows", within)
        common = (step, last, step == 0, idx, place)
        rest = filter_call(
            rest_kernel, "filter_rest", *common, rest_parts, ["near", "mid", "far"], near_halo, rounded, current, older, last
        )
        far = filter_call(
            far_kernel, "filter_far", *common, far_parts, ["far", "mid"], far_halo, rounded, current, older, False
        )
        if last:
            return rest, far[0]
        older = current
        current = dict(near=rest[0], mid=rest[1], far=far[0])
        rounded = dict(near=rest[2], mid=rest[3], far=far[1])
        near_out, far_out = rounded["near"], rounded["far"]


PAIRS = [(i, j) for i in range(8) for j in range(i, 8)]
HALF = len(PAIRS) // 2


def actual(label, core):
    return label + core * (3 - 2 * label)


def label_pairs(rows, vecs, shift, keep):
    pairs = [(row, i, (i + shift) % vecs) for row in range(rows) for i in range(vecs)]
    return [
        (row * vecs + actual(i, row % 2), row * vecs + actual(j, row % 2)) for row, i, j in pairs if keep(j)
    ]


def gram_kernel(total_rows, place, *refs):
    early, late = refs[0:4], refs[4:8]
    keep, send, next1, next2, next3, f, g, sems, out_sems = refs[8:]
    core, label = place[1], place[2]

    def loads(pieces):
        return [
            pltpu.make_async_copy(pieces[s], f.at[actual(lax.rem(label + 4 - s, 4), core)], sems.at[s]) for s in range(4)
        ]

    @pl.when(label == 0)
    def _():
        for copy in loads(late):
            copy.start()

    @pl.when(label != 0)
    def _():
        for copy in loads(early):
            copy.start()

    for copy in loads(early):
        copy.wait()
    copies = [
        pltpu.make_async_copy(f.at[actual(lax.rem(label + s + r, 4), core)], out.at[r - 1], out_sems.at[3 * s + r - 2])
        for s, out in ((1, next1), (2, next2), (3, next3))
        for r in (1, 2, 3)
    ]
    for copy in copies:
        copy.start()
    depth = 8 * SIZE
    width = f.shape[-1]
    for a in range(4):
        left = f[a].reshape(depth, width).T
        for b in range(a, 4):
            tile = jnp.dot(left, f[b].reshape(depth, width), preferred_element_type=F32) * (1.0 / total_rows)
            for i in range(2):
                for j in range(2):
                    if 2 * a + i <= 2 * b + j:
                        n = PAIRS.index((2 * a + i, 2 * b + j))
                        g[n // HALF, n % HALF] = tile[i * SIZE : (i + 1) * SIZE, j * SIZE : (j + 1) * SIZE]
    copies.append(pltpu.make_async_copy(g.at[core], keep, out_sems.at[0]))
    copies.append(pltpu.make_async_copy(g.at[1 - core], send, out_sems.at[1]))
    for copy in copies[-2:]:
        copy.start()
    for copy in copies:
        copy.wait()


def gram(total_rows, place, early, late):
    width = early[0].shape[-1]
    half = jax.ShapeDtypeStruct((HALF, SIZE, SIZE), F32)
    return pl.pallas_call(
        functools.partial(gram_kernel, total_rows),
        out_shape=[half, half] + [jax.ShapeDtypeStruct((3, 8, SIZE, width), BF)] * 3,
        grid_spec=pltpu.PrefetchScalarGridSpec(
            num_scalar_prefetch=1,
            grid=(),
            in_specs=[ANY] * 8,
            out_specs=[ANY] * 5,
            scratch_shapes=[
                pltpu.VMEM((4, 8, SIZE, width), BF),
                pltpu.VMEM((2, HALF, SIZE, SIZE), F32),
                pltpu.SemaphoreType.DMA((4,)),
                pltpu.SemaphoreType.DMA((11,)),
            ],
        ),
        compiler_params=params(24),
        cost_estimate=pl.CostEstimate(flops=10 * 2 * 1024 * 256 * 256, bytes_accessed=8 * MIB, transcendentals=0),
        name="gram",
    )(place, *early, *late)


def sum_everywhere(keep, send):
    rows = lax.axis_size("rows")
    vecs = lax.axis_size("vecs")
    swap = [(i, i ^ 1) for i in range(rows)]
    groups = [list(range(c, rows, 2)) for c in range(2)]
    count = rows // 2
    mine = keep + lax.ppermute(send, "rows", swap)
    parts = mine.reshape(count, -1, mine.shape[-1])
    parts = lax.all_to_all(parts, "rows", 0, 0, axis_index_groups=groups, tiled=True)
    part = jnp.sum(parts, axis=0)
    others = [lax.ppermute(part, "vecs", [(i, (i + s) % vecs) for i in range(vecs)]) for s in range(1, vecs)]
    part = part + sum(others)
    spread_out = jnp.broadcast_to(part[None], (count,) + part.shape)
    mine = lax.all_to_all(spread_out, "rows", 0, 0, axis_index_groups=groups, tiled=True).reshape(keep.shape)
    return mine, lax.ppermute(mine, "rows", swap)


def recip(x):
    return pl.reciprocal(x, approx=True)


def inv_sqrt(x):
    y = lax.rsqrt(x)
    return y * (1.5 - 0.5 * x * (y * y))


def spread(x):
    return jnp.broadcast_to(x, (8, SIZE))


def tree_sum(terms):
    while len(terms) > 1:
        terms = [terms[i] + terms[i + 1] if i + 1 < len(terms) else terms[i] for i in range(0, len(terms), 2)]
    return terms[0]


def eliminate(rows):
    count = len(rows)
    lane = lax.broadcasted_iota(jnp.int32, (8, SIZE), 1)
    sub = lax.broadcasted_iota(jnp.int32, (8, SIZE), 0)
    done = []
    for k in range(count):
        base = 8 * k
        inside = (lane >= base) & (lane < base + 8)
        cols = {(q, i): spread(rows[i][:, base + q : base + q + 1]) for i in range(k, count) for q in range(8)}
        s = {(r, q): spread(cols[q, k][r : r + 1, :]) for r in range(8) for q in range(r + 1)}
        own = jnp.where(inside, jnp.where(lane == base + sub, 1.0, 0.0), rows[k])
        row = [spread(own[q : q + 1, :]) for q in range(8)]
        inv = {}
        m = {}
        for j in range(8):
            inv[j] = recip(s[j, j])
            for i in range(j + 1, 8):
                m[i, j] = s[i, j] * inv[j]
            for i in range(j + 1, 8):
                for t in range(j + 1, i + 1):
                    term = (s[i, j] * s[t, j]) * inv[j] if i == t else m[i, j] * s[t, j]
                    s[i, t] = s[i, t] - term
                row[i] = row[i] - m[i, j] * row[j]
        out = None
        for p in range(8):
            scaled = row[p] * inv_sqrt(s[p, p])
            out = scaled if out is None else jnp.where(sub == p, scaled, out)
        done.append(jnp.where(lane <= base + sub, out, 0.0))
        z = [row[p] * inv[p] for p in range(8)]
        for q in range(6, -1, -1):
            for p in range(7, q, -1):
                z[q] = z[q] - m[p, q] * z[p]
        for i in range(k + 1, count):
            rows[i] = jnp.where(inside, 0.0, rows[i]) - tree_sum([cols[q, i] * z[q] for q in range(8)])
    return done


def split3(value):
    high = value.astype(BF)
    rest = value - high.astype(F32)
    mid = rest.astype(BF)
    return high, mid, (rest - mid.astype(F32)).astype(BF)


def factor_kernel(place, mine, other, high_ref, low_ref, w, diag, following, left, right, sems):
    n = 8
    x, core, label = place[0], place[1], place[2]
    at = lambda i: pl.ds(pl.multiple_of(i * SIZE, SIZE), SIZE)
    exact = functools.partial(jnp.dot, preferred_element_type=F32, precision=EXACT)

    def copies(halves):
        return [
            pltpu.make_async_copy(
                halves[m // HALF].at[m % HALF], w.at[pl.ds(SIZE * i, SIZE), pl.ds(SIZE * j, SIZE)], sems.at[m]
            )
            for m, (i, j) in enumerate(PAIRS)
        ]

    @pl.when(core == 0)
    def _():
        for copy in copies([mine, other]):
            copy.start()

    @pl.when(core == 1)
    def _():
        for copy in copies([other, mine]):
            copy.start()

    diag[...] = jnp.zeros(diag.shape, F32)
    left[...] = jnp.zeros(left.shape, BF)
    for copy in copies([mine, other]):
        copy.wait()
    for i in range(1, n):
        w[pl.ds(SIZE * i, SIZE), pl.ds(0, SIZE * i)] = jnp.zeros((SIZE, SIZE * i), F32)
    w[pl.ds(n * SIZE, (n - 1) * SIZE), :] = jnp.zeros(((n - 1) * SIZE, n * SIZE), F32)
    following[...] = w[pl.ds(0, SIZE), pl.ds(0, SIZE)]

    def step(k, _):
        done = eliminate([following[pl.ds(8 * r, 8), :] for r in range(16)])
        p = jnp.maximum(k - 1, 0)
        x_prev = diag[...]
        w[at(p), :] = jnp.where(k > 0, exact(x_prev, w[at(p), :]), w[at(p), :])
        w[at(p), at(p)] = jnp.where(k > 0, x_prev, w[at(p), at(p)])
        high, mid, low = split3(jnp.where(k > 0, w[at(p), :], 0.0))
        for t, v in enumerate((high, mid, low, high, mid, high)):
            right[pl.ds(SIZE * t, SIZE), :] = v
        for c in range(n):
            cut = slice(SIZE * c, SIZE * c + SIZE)
            high_t, mid_t, low_t = high[:, cut].T, mid[:, cut].T, low[:, cut].T
            for t, v in enumerate((high_t, high_t, high_t, mid_t, mid_t, low_t)):
                left[pl.ds(SIZE * c, SIZE), pl.ds(SIZE * t, SIZE)] = v
        for t in range(n - 1):
            w[at(k + t), at(p)] = jnp.zeros((SIZE, SIZE), F32)
        for t in range(n - 1):
            w[at(k + t), :] = w[at(k + t), :] - jnp.dot(left[at(k + t), :], right[...], preferred_element_type=F32)
        for r in range(16):
            diag[pl.ds(8 * r, 8), :] = done[r]
        q = jnp.minimum(k + 1, n - 1)
        ahead = exact(diag[...], w[at(k), at(q)])
        following[...] = w[at(q), at(q)] - exact(ahead.T, ahead)
        return 0

    lax.fori_loop(0, n, step, 0)
    end = pl.ds((n - 1) * SIZE, SIZE)
    w[end, :] = exact(diag[...], w[end, :])
    w[end, end] = diag[...]
    for r in range(2):
        row = 2 * x + r
        for c in range(n):
            column = 2 * actual(lax.rem(label + c // 2, 4), core) + c % 2
            value = jnp.where(column <= row, w[at(row), at(column)], 0.0)
            high = value.astype(BF)
            high_ref[pl.ds(SIZE * r, SIZE), pl.ds(SIZE * c, SIZE)] = high
            low_ref[pl.ds(SIZE * r, SIZE), pl.ds(SIZE * c, SIZE)] = (value - high.astype(F32)).astype(BF)


def factor(place, mine, other):
    n = 8
    vmem = pl.BlockSpec(memory_space=pltpu.VMEM)
    return pl.pallas_call(
        factor_kernel,
        out_shape=[jax.ShapeDtypeStruct((2 * SIZE, n * SIZE), BF)] * 2,
        grid_spec=pltpu.PrefetchScalarGridSpec(
            num_scalar_prefetch=1,
            grid=(),
            in_specs=[ANY] * 2,
            out_specs=[vmem] * 2,
            scratch_shapes=[
                pltpu.VMEM(((2 * n - 1) * SIZE, n * SIZE), F32),
                pltpu.VMEM((SIZE, SIZE), F32),
                pltpu.VMEM((SIZE, SIZE), F32),
                pltpu.VMEM(((2 * n - 1) * SIZE, 6 * SIZE), BF),
                pltpu.VMEM((6 * SIZE, n * SIZE), BF),
                pltpu.SemaphoreType.DMA((len(PAIRS),)),
            ],
        ),
        compiler_params=params(32),
        cost_estimate=pl.CostEstimate(flops=1_000_000, bytes_accessed=4 * MIB, transcendentals=0),
        name="factor",
    )(place, mine, other)


def apply_kernel(place, *refs):
    early, got_early, late, got_late, far = refs[0:4], refs[4:7], refs[7], refs[8:11], refs[11:14]
    high, low, out, tiles, sems = refs[14:]
    core, label = place[1], place[2]
    t = pl.program_id(0)
    steps = pl.num_programs(0)
    per = late.shape[0]
    width = late.shape[-1]
    slot = lax.rem(t, 2)

    def copies(slot, t):
        return [
            pltpu.make_async_copy(
                tiles.at[slot, s], out.at[actual(lax.rem(label + 4 - s, 4), core), pl.ds(t * per, per)], sems.at[slot, s]
            )
            for s in range(4)
        ]

    @pl.when(t >= 2)
    def _():
        for copy in copies(slot, t - 2):
            copy.wait()

    dims = (((1,), (1,)), ((), ()))
    for s in range(4):
        own = jnp.where(lax.rem(label + 4 - s, 4) == 0, late[...], early[(4 - s) % 4][...])
        if s == 0:
            panels = [own] + [jnp.where(label == 0, got_late[r][...], got_early[r][...]) for r in (2, 1, 0)]
        else:
            panels = [own] + [far[s - 1][r] for r in range(3)]
        left = jnp.concatenate([p.reshape(per * SIZE, width) for p in panels], axis=1)
        value = lax.dot_general(left, high[...], dims, preferred_element_type=F32)
        value = value + lax.dot_general(left, low[...], dims, preferred_element_type=F32)
        tiles[slot, s] = value.reshape(per, SIZE, width)
    for copy in copies(slot, t):
        copy.start()

    @pl.when(t == steps - 1)
    def _():
        for copy in copies(1 - slot, t - 1) + copies(slot, t):
            copy.wait()


def apply(place, early, got_early, late, got_late, far, high, low):
    width = late.shape[-1]
    per = 2
    whole = pl.BlockSpec(high.shape, lambda t, *_: (0, 0))
    rows = pl.BlockSpec((per, SIZE, width), lambda t, *_: (t, 0, 0))
    return pl.pallas_call(
        apply_kernel,
        out_shape=jax.ShapeDtypeStruct((4, 8, SIZE, width), F32),
        grid_spec=pltpu.PrefetchScalarGridSpec(
            num_scalar_prefetch=1,
            grid=(8 // per,),
            in_specs=[rows] * 11 + [pl.BlockSpec((3, per, SIZE, width), lambda t, *_: (0, t, 0, 0))] * 3 + [whole, whole],
            out_specs=ANY,
            scratch_shapes=[pltpu.VMEM((2, 4, per, SIZE, width), F32), pltpu.SemaphoreType.DMA((2, 4))],
        ),
        compiler_params=params(32),
        cost_estimate=pl.CostEstimate(flops=4 * 1024 * 1024 * 256 * 4, bytes_accessed=14 * MIB, transcendentals=0),
        name="apply",
    )(place, *early, *got_early, late, *got_late, *far, high, low)


def shards(vectors, blocks, columns):
    block_rows = blocks.shape[0]
    width = vectors.shape[1]
    row = lax.axis_index("rows")
    x = lax.axis_index("vecs")
    vecs = lax.axis_size("vecs")
    total_rows = vectors.shape[0] * lax.axis_size("rows")
    idx = columns - row * block_rows + REACH
    core = lax.rem(row, 2)
    label = actual(x, core)
    place = jnp.stack([x, core, label]).astype(jnp.int32)
    early, late = chebyshev(vectors.reshape(block_rows, SIZE, width), blocks, idx, place)
    rows = lax.axis_size("rows")

    def shift(a, s, keep):
        return lax.ppermute(a, ("rows", "vecs"), label_pairs(rows, vecs, s, keep))

    got_early = [shift(early[s], s, lambda j: j != 0) for s in range(1, vecs)]
    got_late = [shift(late, s, lambda j: j == 0) for s in range(1, vecs)]
    keep, send, *following = gram(total_rows, place, [early[0]] + got_early, [late] + got_late)
    mine, other = sum_everywhere(keep, send)
    far = [shift(following[s - 1], s, lambda j: True) for s in range(1, vecs)]
    inverse_high, inverse_low = factor(place, mine, other)
    return apply(place, early, got_early, late, got_late, far, inverse_high, inverse_low).reshape(vectors.shape)


def solution(mesh):
    in_specs = (P("rows", "vecs"), P("rows", None, None, None), P("rows", None))
    out_specs = P("rows", "vecs")
    return jax.shard_map(shards, mesh=mesh, in_specs=in_specs, out_specs=out_specs, check_vma=False)
```

```python
import functools

import jax
import jax.numpy as jnp
from jax import lax
from jax.experimental import pallas as pl
from jax.experimental.pallas import tpu as pltpu
from jax.sharding import PartitionSpec as P

DEGREE = 4
filter_center = 0.25
filter_radius = 1.25

F32 = jnp.float32
BF = jnp.bfloat16
EXACT = lax.Precision.HIGHEST
SIZE = 128
REACH = 8
MIB = 1 << 20

ANY = pl.BlockSpec(memory_space=pl.ANY)


def params(mib):
    return pltpu.CompilerParams(vmem_limit_bytes=mib * MIB)


def load_all(pairs, sems):
    copies = [pltpu.make_async_copy(src, dst, sems.at[n]) for n, (src, dst) in enumerate(pairs)]
    for copy in copies:
        copy.start()
    for copy in copies:
        copy.wait()


def row_product(idx, row, shift, blocks_ref, r, pad):
    count = blocks_ref.shape[1]
    left = jnp.concatenate([blocks_ref[r, j] for j in range(count)], axis=1)
    right = jnp.concatenate([pad[idx[row, j] - shift] for j in range(count)], axis=0)
    return jnp.dot(left, right, preferred_element_type=F32)


def recurrence(step, product, current, older):
    scale = (2.0 if step else 1.0) / filter_radius
    newer = scale * product - (scale * filter_center) * current.astype(F32)
    return newer - older.astype(F32) if step else newer


def far_kernel(step, last, source_at, idx, place, *refs):
    refs = list(refs)
    take = lambda n: [refs.pop(0) for _ in range(n)]
    (blocks,) = take(1)
    halo, far, mid = take(3)
    (current,) = take(1)
    older = take(1)[0] if step else None
    if last:
        near_new, mid_new = take(2)
        sends = take(4)
        pad, sems, rounded, out_sems = take(4)
    else:
        fresh, rounded = take(2)
        pad, sems = take(2)
    g = pl.program_id(0)
    per = blocks.shape[0]
    core = place[1]
    far_at = 24 * core if source_at else 0
    mid_at = 8 if source_at else 0

    @pl.when(g == 0)
    def _():
        load_all(
            [
                (halo, pad.at[pl.ds(16 * core, 8)]),
                (far.at[pl.ds(far_at, 8)], pad.at[pl.ds(8, 8)]),
                (mid.at[pl.ds(mid_at + 8 * core, 8)], pad.at[pl.ds(16 * (1 - core), 8)]),
            ],
            sems,
        )

    for r in range(per):
        product = row_product(idx, 24 * core + g * per + r, 24 * core, blocks, r, pad)
        newer = recurrence(step, product, current[r], older[r] if step else None)
        if last:
            rounded[g * per + r] = newer.astype(BF)
        else:
            fresh[r] = newer
            rounded[r] = newer.astype(BF)

    if last:

        @pl.when(g == pl.num_programs(0) - 1)
        def _():
            sources = {
                0: [rounded, mid_new.at[pl.ds(0, 8)], mid_new.at[pl.ds(8, 8)], near_new],
                1: [near_new, mid_new.at[pl.ds(0, 8)], mid_new.at[pl.ds(8, 8)], rounded],
            }
            for s in range(4):
                for q in range(4):
                    for c in range(2):

                        @pl.when((lax.rem(place[0] + s, 4) == q) & (core == c))
                        def _():
                            pltpu.make_async_copy(sources[c][q], sends[s], out_sems.at[s]).start()

            for s in range(4):
                pltpu.make_async_copy(rounded, sends[s], out_sems.at[s]).wait()


def rest_kernel(step, last, source_at, idx, place, *refs):
    refs = list(refs)
    take = lambda n: [refs.pop(0) for _ in range(n)]
    blocks = take(2)
    halo, near, mid, far = take(4)
    current = take(2)
    older = take(2) if step else None
    fresh = None if last else take(2)
    rounded = take(2)
    pad, sems = take(2)
    g = pl.program_id(0)
    core = place[1]
    near_at = 24 * (1 - core)
    far_at = 24 * core

    @pl.when(g == 0)
    def _():
        load_all(
            [
                (halo, pad.at[pl.ds(40 * (1 - core), 8)]),
                (near.at[pl.ds(near_at if source_at else 0, 8)], pad.at[pl.ds(8 + near_at, 8)]),
                (mid.at[pl.ds(8 if source_at else 0, 16)], pad.at[pl.ds(16, 16)]),
                (far.at[pl.ds(far_at if source_at else 0, 8)], pad.at[pl.ds(8 + far_at, 8)]),
            ],
            sems,
        )

    for n, first in enumerate((near_at, 8)):
        per = blocks[n].shape[0]
        for r in range(per):
            product = row_product(idx, first + g * per + r, 0, blocks[n], r, pad)
            newer = recurrence(step, product, current[n][r], older[n][r] if step else None)
            if not last:
                fresh[n][r] = newer
            rounded[n][r] = newer.astype(BF)


def filter_call(kernel, name, step, last, source_at, idx, place, parts, moved, halo, rounded, current, older, extra):
    width = halo.shape[-1]
    nnz = parts["blocks"].shape[1]
    blocks = parts["blocks"]
    in_specs, operands, shapes, out_specs = [], [], [], []
    groups = parts["groups"]
    for key, count, per, first in groups:
        in_specs.append(
            pl.BlockSpec((per, nnz, SIZE, SIZE), lambda g, idx, place, per=per, first=first: (g + first(place[1]) // per, 0, 0, 0))
        )
        operands.append(blocks)
    in_specs += [ANY] * (1 + len(moved))
    operands += [halo] + [rounded[key] for key in moved]
    for arrays in [current] + ([older] if step else []):
        at = arrays.get("whole", False)
        for key, count, per, first in groups:
            index = (
                (lambda g, idx, place, per=per, first=first: (g + first(place[1]) // per, 0, 0))
                if at
                else (lambda g, idx, place: (g, 0, 0))
            )
            in_specs.append(pl.BlockSpec((per, SIZE, width), index))
            operands.append(arrays[key])
    scratch = [pltpu.VMEM((parts["window"], SIZE, width), BF), pltpu.SemaphoreType.DMA((1 + len(moved),))]
    for kind in (F32, BF):
        if kind is F32 and last:
            continue
        for key, count, per, first in groups:
            shapes.append(jax.ShapeDtypeStruct((count, SIZE, width), kind))
            out_specs.append(pl.BlockSpec((per, SIZE, width), lambda g, idx, place: (g, 0, 0)))
    if extra:
        in_specs += [ANY] * len(extra)
        operands += extra
        shapes = [jax.ShapeDtypeStruct((8, SIZE, width), BF)] * 4
        out_specs = [ANY] * 4
        scratch += [pltpu.VMEM((8, SIZE, width), BF), pltpu.SemaphoreType.DMA((4,))]
    total = sum(count for _, count, _, _ in groups)
    return pl.pallas_call(
        functools.partial(kernel, step, last, source_at),
        out_shape=shapes,
        grid_spec=pltpu.PrefetchScalarGridSpec(
            num_scalar_prefetch=2,
            grid=(4,),
            in_specs=in_specs,
            out_specs=out_specs,
            scratch_shapes=scratch,
        ),
        compiler_params=params(24),
        cost_estimate=pl.CostEstimate(
            flops=total * nnz * 2 * SIZE * SIZE * width, bytes_accessed=total * MIB // 2, transcendentals=0
        ),
        name=name,
    )(idx, place, *operands)


def chebyshev(vectors, blocks, idx, place):
    rows = lax.axis_size("rows")
    core = place[1]
    within = [(i, i ^ 1) for i in range(rows)]
    between = [(i, i + 1 if i % 2 else i - 1) for i in range(1, rows - 1)]
    far_group = ("far", 8, 2, lambda c: 24 * c)
    near_group = ("near", 8, 2, lambda c: 24 * (1 - c))
    mid_group = ("mid", 16, 4, lambda c: 8)
    far_parts = dict(blocks=blocks, groups=[far_group], window=24)
    rest_parts = dict(blocks=blocks, groups=[near_group, mid_group], window=48)
    start = dict(near=vectors, mid=vectors, far=vectors, whole=True)
    rounded = current = start
    older = None
    far_out = lax.dynamic_slice_in_dim(vectors, 24 * core, 8, 0)
    near_out = lax.dynamic_slice_in_dim(vectors, 24 * (1 - core), 8, 0)
    for step in range(DEGREE):
        last = step == DEGREE - 1
        far_halo = lax.ppermute(far_out, "rows", between)
        near_halo = lax.ppermute(near_out, "rows", within)
        common = (step, last, step == 0, idx, place)
        rest = filter_call(
            rest_kernel, "filter_rest", *common, rest_parts, ["near", "mid", "far"], near_halo, rounded, current, older, None
        )
        extra = rest if last else None
        far = filter_call(
            far_kernel, "filter_far", *common, far_parts, ["far", "mid"], far_halo, rounded, current, older, extra
        )
        if last:
            return far
        older = current
        current = dict(near=rest[0], mid=rest[1], far=far[0])
        rounded = dict(near=rest[2], mid=rest[3], far=far[1])
        near_out, far_out = rounded["near"], rounded["far"]


PAIRS = [(i, j) for i in range(8) for j in range(i, 8)]
HALF = len(PAIRS) // 2


def gram_kernel(total_rows, place, own, got1, got2, got3, keep, send, next1, next2, next3, f, g, sems, out_sems):
    pieces = [own, got1, got2, got3]
    x, core = place[0], place[1]
    load_all([(pieces[s], f.at[lax.rem(x + 4 - s, 4)]) for s in range(4)], sems)
    copies = [
        pltpu.make_async_copy(f.at[lax.rem(x + s + r, 4)], out.at[r - 1], out_sems.at[3 * s + r - 2])
        for s, out in ((1, next1), (2, next2), (3, next3))
        for r in (1, 2, 3)
    ]
    for copy in copies:
        copy.start()
    depth = 8 * SIZE
    width = f.shape[-1]
    for a in range(4):
        left = f[a].reshape(depth, width).T
        for b in range(a, 4):
            tile = jnp.dot(left, f[b].reshape(depth, width), preferred_element_type=F32) * (1.0 / total_rows)
            for i in range(2):
                for j in range(2):
                    if 2 * a + i <= 2 * b + j:
                        n = PAIRS.index((2 * a + i, 2 * b + j))
                        g[n // HALF, n % HALF] = tile[i * SIZE : (i + 1) * SIZE, j * SIZE : (j + 1) * SIZE]
    copies.append(pltpu.make_async_copy(g.at[core], keep, out_sems.at[0]))
    copies.append(pltpu.make_async_copy(g.at[1 - core], send, out_sems.at[1]))
    for copy in copies[-2:]:
        copy.start()
    for copy in copies:
        copy.wait()


def gram(total_rows, place, own, got):
    width = own.shape[-1]
    half = jax.ShapeDtypeStruct((HALF, SIZE, SIZE), F32)
    return pl.pallas_call(
        functools.partial(gram_kernel, total_rows),
        out_shape=[half, half] + [jax.ShapeDtypeStruct((3, 8, SIZE, width), BF)] * 3,
        grid_spec=pltpu.PrefetchScalarGridSpec(
            num_scalar_prefetch=1,
            grid=(),
            in_specs=[ANY] * 4,
            out_specs=[ANY] * 5,
            scratch_shapes=[
                pltpu.VMEM((4, 8, SIZE, width), BF),
                pltpu.VMEM((2, HALF, SIZE, SIZE), F32),
                pltpu.SemaphoreType.DMA((4,)),
                pltpu.SemaphoreType.DMA((11,)),
            ],
        ),
        compiler_params=params(24),
        cost_estimate=pl.CostEstimate(flops=10 * 2 * 1024 * 256 * 256, bytes_accessed=8 * MIB, transcendentals=0),
        name="gram",
    )(place, own, *got)


def sum_everywhere(keep, send):
    rows = lax.axis_size("rows")
    vecs = lax.axis_size("vecs")
    swap = [(i, i ^ 1) for i in range(rows)]
    groups = [list(range(c, rows, 2)) for c in range(2)]
    count = rows // 2
    mine = keep + lax.ppermute(send, "rows", swap)
    parts = mine.reshape(count, -1, mine.shape[-1])
    parts = lax.all_to_all(parts, "rows", 0, 0, axis_index_groups=groups, tiled=True)
    part = jnp.sum(parts, axis=0)
    others = [lax.ppermute(part, "vecs", [(i, (i + s) % vecs) for i in range(vecs)]) for s in range(1, vecs)]
    part = part + sum(others)
    spread_out = jnp.broadcast_to(part[None], (count,) + part.shape)
    mine = lax.all_to_all(spread_out, "rows", 0, 0, axis_index_groups=groups, tiled=True).reshape(keep.shape)
    return mine, lax.ppermute(mine, "rows", swap), part


def recip(x):
    return pl.reciprocal(x, approx=True)


def inv_sqrt(x):
    y = lax.rsqrt(x)
    return y * (1.5 - 0.5 * x * (y * y))


def spread(x):
    return jnp.broadcast_to(x, (8, SIZE))


def tree_sum(terms):
    while len(terms) > 1:
        terms = [terms[i] + terms[i + 1] if i + 1 < len(terms) else terms[i] for i in range(0, len(terms), 2)]
    return terms[0]


def eliminate(rows):
    count = len(rows)
    lane = lax.broadcasted_iota(jnp.int32, (8, SIZE), 1)
    sub = lax.broadcasted_iota(jnp.int32, (8, SIZE), 0)
    done = []
    for k in range(count):
        base = 8 * k
        inside = (lane >= base) & (lane < base + 8)
        cols = {(q, i): spread(rows[i][:, base + q : base + q + 1]) for i in range(k, count) for q in range(8)}
        s = {(r, q): spread(cols[q, k][r : r + 1, :]) for r in range(8) for q in range(r + 1)}
        own = jnp.where(inside, jnp.where(lane == base + sub, 1.0, 0.0), rows[k])
        row = [spread(own[q : q + 1, :]) for q in range(8)]
        inv = {}
        m = {}
        for j in range(8):
            inv[j] = recip(s[j, j])
            for i in range(j + 1, 8):
                m[i, j] = s[i, j] * inv[j]
            for i in range(j + 1, 8):
                for t in range(j + 1, i + 1):
                    term = (s[i, j] * s[t, j]) * inv[j] if i == t else m[i, j] * s[t, j]
                    s[i, t] = s[i, t] - term
                row[i] = row[i] - m[i, j] * row[j]
        out = None
        for p in range(8):
            scaled = row[p] * inv_sqrt(s[p, p])
            out = scaled if out is None else jnp.where(sub == p, scaled, out)
        done.append(jnp.where(lane <= base + sub, out, 0.0))
        z = [row[p] * inv[p] for p in range(8)]
        for q in range(6, -1, -1):
            for p in range(7, q, -1):
                z[q] = z[q] - m[p, q] * z[p]
        for i in range(k + 1, count):
            rows[i] = jnp.where(inside, 0.0, rows[i]) - tree_sum([cols[q, i] * z[q] for q in range(8)])
    return done


def split3(value):
    high = value.astype(BF)
    rest = value - high.astype(F32)
    mid = rest.astype(BF)
    return high, mid, (rest - mid.astype(F32)).astype(BF)


def factor_kernel(place, mine, other, high_ref, low_ref, w, diag, following, left, right, sems):
    n = 8
    x, core = place[0], place[1]
    at = lambda i: pl.ds(pl.multiple_of(i * SIZE, SIZE), SIZE)
    exact = functools.partial(jnp.dot, preferred_element_type=F32, precision=EXACT)

    def copies(halves):
        return [
            pltpu.make_async_copy(
                halves[m // HALF].at[m % HALF], w.at[pl.ds(SIZE * i, SIZE), pl.ds(SIZE * j, SIZE)], sems.at[m]
            )
            for m, (i, j) in enumerate(PAIRS)
        ]

    @pl.when(core == 0)
    def _():
        for copy in copies([mine, other]):
            copy.start()

    @pl.when(core == 1)
    def _():
        for copy in copies([other, mine]):
            copy.start()

    diag[...] = jnp.zeros(diag.shape, F32)
    left[...] = jnp.zeros(left.shape, BF)
    for copy in copies([mine, other]):
        copy.wait()
    for i in range(1, n):
        w[pl.ds(SIZE * i, SIZE), pl.ds(0, SIZE * i)] = jnp.zeros((SIZE, SIZE * i), F32)
    w[pl.ds(n * SIZE, (n - 1) * SIZE), :] = jnp.zeros(((n - 1) * SIZE, n * SIZE), F32)
    following[...] = w[pl.ds(0, SIZE), pl.ds(0, SIZE)]

    def step(k, _):
        done = eliminate([following[pl.ds(8 * r, 8), :] for r in range(16)])
        p = jnp.maximum(k - 1, 0)
        x_prev = diag[...]
        w[at(p), :] = jnp.where(k > 0, exact(x_prev, w[at(p), :]), w[at(p), :])
        w[at(p), at(p)] = jnp.where(k > 0, x_prev, w[at(p), at(p)])
        high, mid, low = split3(jnp.where(k > 0, w[at(p), :], 0.0))
        for t, v in enumerate((high, mid, low, high, mid, high)):
            right[pl.ds(SIZE * t, SIZE), :] = v
        for c in range(n):
            cut = slice(SIZE * c, SIZE * c + SIZE)
            high_t, mid_t, low_t = high[:, cut].T, mid[:, cut].T, low[:, cut].T
            for t, v in enumerate((high_t, high_t, high_t, mid_t, mid_t, low_t)):
                left[pl.ds(SIZE * c, SIZE), pl.ds(SIZE * t, SIZE)] = v
        for t in range(n - 1):
            w[at(k + t), at(p)] = jnp.zeros((SIZE, SIZE), F32)
        for t in range(n - 1):
            w[at(k + t), :] = w[at(k + t), :] - jnp.dot(left[at(k + t), :], right[...], preferred_element_type=F32)
        for r in range(16):
            diag[pl.ds(8 * r, 8), :] = done[r]
        q = jnp.minimum(k + 1, n - 1)
        ahead = exact(diag[...], w[at(k), at(q)])
        following[...] = w[at(q), at(q)] - exact(ahead.T, ahead)
        return 0

    lax.fori_loop(0, n, step, 0)
    end = pl.ds((n - 1) * SIZE, SIZE)
    w[end, :] = exact(diag[...], w[end, :])
    w[end, end] = diag[...]
    for r in range(2):
        row = 2 * x + r
        for c in range(n):
            column = 2 * lax.rem(x + c // 2, 4) + c % 2
            value = jnp.where(column <= row, w[at(row), at(column)], 0.0)
            value = value.T
            high = value.astype(BF)
            high_ref[pl.ds(SIZE * c, SIZE), pl.ds(SIZE * r, SIZE)] = high
            low_ref[pl.ds(SIZE * c, SIZE), pl.ds(SIZE * r, SIZE)] = (value - high.astype(F32)).astype(BF)


def factor(place, mine, other):
    n = 8
    vmem = pl.BlockSpec(memory_space=pltpu.VMEM)
    return pl.pallas_call(
        factor_kernel,
        out_shape=[jax.ShapeDtypeStruct((n * SIZE, 2 * SIZE), BF)] * 2,
        grid_spec=pltpu.PrefetchScalarGridSpec(
            num_scalar_prefetch=1,
            grid=(),
            in_specs=[ANY] * 2,
            out_specs=[vmem] * 2,
            scratch_shapes=[
                pltpu.VMEM(((2 * n - 1) * SIZE, n * SIZE), F32),
                pltpu.VMEM((SIZE, SIZE), F32),
                pltpu.VMEM((SIZE, SIZE), F32),
                pltpu.VMEM(((2 * n - 1) * SIZE, 6 * SIZE), BF),
                pltpu.VMEM((6 * SIZE, n * SIZE), BF),
                pltpu.SemaphoreType.DMA((len(PAIRS),)),
            ],
        ),
        compiler_params=params(32),
        cost_estimate=pl.CostEstimate(flops=1_000_000, bytes_accessed=4 * MIB, transcendentals=0),
        name="factor",
    )(place, mine, other)


def apply_kernel(place, *refs):
    own, got, far = refs[0:4], refs[4:7], refs[7:10]
    high, low, out, tiles, sems = refs[10:]
    x = place[0]
    t = pl.program_id(0)
    steps = pl.num_programs(0)
    per = own[0].shape[0]
    width = own[0].shape[-1]
    slot = lax.rem(t, 2)

    def copies(slot, t):
        return [
            pltpu.make_async_copy(
                tiles.at[slot, s], out.at[lax.rem(x + 4 - s, 4), pl.ds(t * per, per)], sems.at[slot, s]
            )
            for s in range(4)
        ]

    @pl.when(t >= 2)
    def _():
        for copy in copies(slot, t - 2):
            copy.wait()

    for s in range(4):
        if s == 0:
            panels = [own[0][...], got[2][...], got[1][...], got[0][...]]
        else:
            panels = [own[4 - s][...]] + [far[s - 1][r] for r in range(3)]
        left = jnp.concatenate([p.reshape(per * SIZE, width) for p in panels], axis=1)
        value = jnp.dot(left, high[...], preferred_element_type=F32)
        value = value + jnp.dot(left, low[...], preferred_element_type=F32)
        tiles[slot, s] = value.reshape(per, SIZE, width)
    for copy in copies(slot, t):
        copy.start()

    @pl.when(t == steps - 1)
    def _():
        for copy in copies(1 - slot, t - 1) + copies(slot, t):
            copy.wait()


def apply(place, own, got, far, high, low):
    width = own[0].shape[-1]
    per = 2
    whole = pl.BlockSpec(high.shape, lambda t, *_: (0, 0))
    rows = pl.BlockSpec((per, SIZE, width), lambda t, *_: (t, 0, 0))
    return pl.pallas_call(
        apply_kernel,
        out_shape=jax.ShapeDtypeStruct((4, 8, SIZE, width), F32),
        grid_spec=pltpu.PrefetchScalarGridSpec(
            num_scalar_prefetch=1,
            grid=(8 // per,),
            in_specs=[rows] * 7 + [pl.BlockSpec((3, per, SIZE, width), lambda t, *_: (0, t, 0, 0))] * 3 + [whole, whole],
            out_specs=ANY,
            scratch_shapes=[pltpu.VMEM((2, 4, per, SIZE, width), F32), pltpu.SemaphoreType.DMA((2, 4))],
        ),
        compiler_params=params(60),
        cost_estimate=pl.CostEstimate(flops=4 * 1024 * 1024 * 256 * 4, bytes_accessed=14 * MIB, transcendentals=0),
        name="apply",
    )(place, *own, *got, *far, high, low)


def shards(vectors, blocks, columns):
    block_rows = blocks.shape[0]
    width = vectors.shape[1]
    row = lax.axis_index("rows")
    x = lax.axis_index("vecs")
    vecs = lax.axis_size("vecs")
    total_rows = vectors.shape[0] * lax.axis_size("rows")
    idx = columns - row * block_rows + REACH
    place = jnp.stack([x, lax.rem(row, 2)]).astype(jnp.int32)
    own = chebyshev(vectors.reshape(block_rows, SIZE, width), blocks, idx, place)
    shift = lambda a, s: lax.ppermute(a, "vecs", [(i, (i + s) % vecs) for i in range(vecs)])
    got = [shift(own[s], s) for s in range(1, vecs)]
    keep, send, *following = gram(total_rows, place, own[0], got)
    mine, other, part = sum_everywhere(keep, send)
    far = [shift(following[s - 1], s) for s in range(1, vecs)]
    inverse_high, inverse_low = factor(place, mine, other)
    return apply(place, own, got, far, inverse_high, inverse_low).reshape(vectors.shape)


def solution(mesh):
    in_specs = (P("rows", "vecs"), P("rows", None, None, None), P("rows", None))
    out_specs = P("rows", "vecs")
    return jax.shard_map(shards, mesh=mesh, in_specs=in_specs, out_specs=out_specs, check_vma=False)
```

```python
import functools

import jax
import jax.numpy as jnp
from jax import lax
from jax.experimental import pallas as pl
from jax.experimental.pallas import tpu as pltpu
from jax.sharding import PartitionSpec as P

DEGREE = 4
filter_center = 0.25
filter_radius = 1.25

F32 = jnp.float32
BF = jnp.bfloat16
EXACT = lax.Precision.HIGHEST
SIZE = 128
REACH = 8
MIB = 1 << 20

ANY = pl.BlockSpec(memory_space=pl.ANY)


def params(mib):
    return pltpu.CompilerParams(vmem_limit_bytes=mib * MIB)


def load_all(pairs, sems):
    copies = [pltpu.make_async_copy(src, dst, sems.at[n]) for n, (src, dst) in enumerate(pairs)]
    for copy in copies:
        copy.start()
    for copy in copies:
        copy.wait()


def row_product(idx, row, shift, blocks_ref, r, pad):
    count = blocks_ref.shape[1]
    left = jnp.concatenate([blocks_ref[r, j] for j in range(count)], axis=1)
    right = jnp.concatenate([pad[idx[row, j] - shift] for j in range(count)], axis=0)
    return jnp.dot(left, right, preferred_element_type=F32)


def recurrence(step, product, current, older):
    scale = (2.0 if step else 1.0) / filter_radius
    newer = scale * product - (scale * filter_center) * current.astype(F32)
    return newer - older.astype(F32) if step else newer


def far_kernel(step, last, whole, idx, place, *refs):
    refs = list(refs)
    take = lambda n: [refs.pop(0) for _ in range(n)]
    blocks, halo, far, mid, current = take(5)
    older = take(1)[0] if step else None
    if last:
        near_new, mid_new = take(2)
        sends = take(4)
        pad, rounded, out_sems = take(3)
    else:
        fresh, rounded, pad = take(3)
    core = place[1]
    first = 24 * core
    far_at = first if whole else 0
    mid_at = (8 if whole else 0) + 8 * core
    pad[pl.ds(16 * core, 8)] = halo[...]
    pad[pl.ds(8, 8)] = far[pl.ds(far_at, 8)]
    pad[pl.ds(16 * (1 - core), 8)] = mid[pl.ds(mid_at, 8)]
    for r in range(8):
        product = row_product(idx, first + r, first, blocks, first + r, pad)
        newer = recurrence(step, product, current[far_at + r], older[(first if step == 1 else 0) + r] if step else None)
        if not last:
            fresh[r] = newer
        rounded[r] = newer.astype(BF)

    if last:
        halves = [mid_new.at[pl.ds(0, 8)], mid_new.at[pl.ds(8, 8)]]
        sources = {0: [rounded] + halves + [near_new], 1: [near_new] + halves + [rounded]}
        for s in range(4):
            for q in range(4):
                for c in range(2):

                    @pl.when((lax.rem(place[0] + s, 4) == q) & (core == c))
                    def _():
                        pltpu.make_async_copy(sources[c][q], sends[s], out_sems.at[s]).start()

        for s in range(4):
            pltpu.make_async_copy(rounded, sends[s], out_sems.at[s]).wait()


def rest_kernel(step, last, whole, idx, place, *refs):
    refs = list(refs)
    take = lambda n: [refs.pop(0) for _ in range(n)]
    blocks, halo, near, mid, far = take(5)
    current = take(2)
    older = take(2) if step else None
    fresh = None if last else take(2)
    rounded = take(2)
    (pad,) = take(1)
    core = place[1]
    near_at = 24 * (1 - core)
    far_at = 24 * core
    pad[pl.ds(40 * (1 - core), 8)] = halo[...]
    pad[pl.ds(8 + near_at, 8)] = near[pl.ds(near_at if whole else 0, 8)]
    pad[pl.ds(16, 16)] = mid[pl.ds(8 if whole else 0, 16)]
    pad[pl.ds(8 + far_at, 8)] = far[pl.ds(far_at if whole else 0, 8)]
    for n, (first, count) in enumerate(((near_at, 8), (8, 16))):
        for r in range(count):
            product = row_product(idx, first + r, 0, blocks, first + r, pad)
            now = current[n][(first if whole else 0) + r]
            before = older[n][(first if step == 1 else 0) + r] if step else None
            newer = recurrence(step, product, now, before)
            if not last:
                fresh[n][r] = newer
            rounded[n][r] = newer.astype(BF)


VMEM = pl.BlockSpec(memory_space=pltpu.VMEM)


def filter_call(kernel, name, step, last, whole, idx, place, blocks, window, groups, moved, halo, rounded, current, older, extra):
    width = halo.shape[-1]
    nnz = blocks.shape[1]
    keys = [key for key, _ in groups]
    operands = [blocks, halo] + [rounded[key] for key in moved] + [current[key] for key in keys]
    if step:
        operands += [older[key] for key in keys]
    operands += extra
    kinds = [BF] if last else [F32, BF]
    shapes = [jax.ShapeDtypeStruct((count, SIZE, width), kind) for kind in kinds for _, count in groups]
    out_specs = [VMEM] * len(shapes)
    scratch = [pltpu.VMEM((window, SIZE, width), BF)]
    if extra:
        shapes = [jax.ShapeDtypeStruct((8, SIZE, width), BF)] * 4
        out_specs = [ANY] * 4
        scratch += [pltpu.VMEM((8, SIZE, width), BF), pltpu.SemaphoreType.DMA((4,))]
    total = sum(count for _, count in groups)
    return pl.pallas_call(
        functools.partial(kernel, step, last, whole),
        out_shape=shapes,
        grid_spec=pltpu.PrefetchScalarGridSpec(
            num_scalar_prefetch=2,
            grid=(),
            in_specs=[VMEM] * len(operands),
            out_specs=out_specs,
            scratch_shapes=scratch,
        ),
        compiler_params=params(30),
        cost_estimate=pl.CostEstimate(
            flops=total * nnz * 2 * SIZE * SIZE * width, bytes_accessed=total * MIB // 2, transcendentals=0
        ),
        name=name,
    )(idx, place, *operands)


def chebyshev(vectors, blocks, idx, place):
    rows = lax.axis_size("rows")
    core = place[1]
    within = [(i, i ^ 1) for i in range(rows)]
    between = [(i, i + 1 if i % 2 else i - 1) for i in range(1, rows - 1)]
    start = dict(near=vectors, mid=vectors, far=vectors)
    rounded = current = start
    older = None
    far_out = lax.dynamic_slice_in_dim(vectors, 24 * core, 8, 0)
    near_out = lax.dynamic_slice_in_dim(vectors, 24 * (1 - core), 8, 0)
    for step in range(DEGREE):
        last = step == DEGREE - 1
        far_halo = lax.ppermute(far_out, "rows", between)
        near_halo = lax.ppermute(near_out, "rows", within)
        common = (step, last, step == 0, idx, place)
        rest = filter_call(
            rest_kernel, "filter_rest", *common, blocks, 48, [("near", 8), ("mid", 16)], ["near", "mid", "far"], near_halo,
            rounded, current, older, [],
        )
        far = filter_call(
            far_kernel, "filter_far", *common, blocks, 24, [("far", 8)], ["far", "mid"], far_halo,
            rounded, current, older, list(rest) if last else [],
        )
        if last:
            return far
        older = current
        current = dict(near=rest[0], mid=rest[1], far=far[0])
        rounded = dict(near=rest[2], mid=rest[3], far=far[1])
        near_out, far_out = rounded["near"], rounded["far"]


PAIRS = [(i, j) for i in range(8) for j in range(i, 8)]
HALF = len(PAIRS) // 2


def gram_kernel(total_rows, place, own, got1, got2, got3, keep, send, next1, next2, next3, f, g, sems, out_sems):
    pieces = [own, got1, got2, got3]
    x, core = place[0], place[1]
    load_all([(pieces[s], f.at[lax.rem(x + 4 - s, 4)]) for s in range(4)], sems)
    copies = [
        pltpu.make_async_copy(f.at[lax.rem(x + s + r, 4)], out.at[r - 1], out_sems.at[3 * s + r - 2])
        for s, out in ((1, next1), (2, next2), (3, next3))
        for r in (1, 2, 3)
    ]
    for copy in copies:
        copy.start()
    depth = 8 * SIZE
    width = f.shape[-1]
    for a in range(4):
        left = f[a].reshape(depth, width).T
        for b in range(a, 4):
            tile = jnp.dot(left, f[b].reshape(depth, width), preferred_element_type=F32) * (1.0 / total_rows)
            for i in range(2):
                for j in range(2):
                    if 2 * a + i <= 2 * b + j:
                        n = PAIRS.index((2 * a + i, 2 * b + j))
                        g[n // HALF, n % HALF] = tile[i * SIZE : (i + 1) * SIZE, j * SIZE : (j + 1) * SIZE]
    copies.append(pltpu.make_async_copy(g.at[core], keep, out_sems.at[0]))
    copies.append(pltpu.make_async_copy(g.at[1 - core], send, out_sems.at[1]))
    for copy in copies[-2:]:
        copy.start()
    for copy in copies:
        copy.wait()


def gram(total_rows, place, own, got):
    width = own.shape[-1]
    half = jax.ShapeDtypeStruct((HALF, SIZE, SIZE), F32)
    return pl.pallas_call(
        functools.partial(gram_kernel, total_rows),
        out_shape=[half, half] + [jax.ShapeDtypeStruct((3, 8, SIZE, width), BF)] * 3,
        grid_spec=pltpu.PrefetchScalarGridSpec(
            num_scalar_prefetch=1,
            grid=(),
            in_specs=[ANY] * 4,
            out_specs=[ANY] * 5,
            scratch_shapes=[
                pltpu.VMEM((4, 8, SIZE, width), BF),
                pltpu.VMEM((2, HALF, SIZE, SIZE), F32),
                pltpu.SemaphoreType.DMA((4,)),
                pltpu.SemaphoreType.DMA((11,)),
            ],
        ),
        compiler_params=params(24),
        cost_estimate=pl.CostEstimate(flops=10 * 2 * 1024 * 256 * 256, bytes_accessed=8 * MIB, transcendentals=0),
        name="gram",
    )(place, own, *got)


def sum_everywhere(keep, send):
    rows = lax.axis_size("rows")
    vecs = lax.axis_size("vecs")
    swap = [(i, i ^ 1) for i in range(rows)]
    groups = [list(range(c, rows, 2)) for c in range(2)]
    count = rows // 2
    mine = keep + lax.ppermute(send, "rows", swap)
    parts = mine.reshape(count, -1, mine.shape[-1])
    parts = lax.all_to_all(parts, "rows", 0, 0, axis_index_groups=groups, tiled=True)
    part = jnp.sum(parts, axis=0)
    others = [lax.ppermute(part, "vecs", [(i, (i + s) % vecs) for i in range(vecs)]) for s in range(1, vecs)]
    part = part + sum(others)
    spread_out = jnp.broadcast_to(part[None], (count,) + part.shape)
    mine = lax.all_to_all(spread_out, "rows", 0, 0, axis_index_groups=groups, tiled=True).reshape(keep.shape)
    return mine, lax.ppermute(mine, "rows", swap), part


def recip(x):
    return pl.reciprocal(x, approx=True)


def inv_sqrt(x):
    y = lax.rsqrt(x)
    return y * (1.5 - 0.5 * x * (y * y))


def spread(x):
    return jnp.broadcast_to(x, (8, SIZE))


def tree_sum(terms):
    while len(terms) > 1:
        terms = [terms[i] + terms[i + 1] if i + 1 < len(terms) else terms[i] for i in range(0, len(terms), 2)]
    return terms[0]


def eliminate(rows):
    count = len(rows)
    lane = lax.broadcasted_iota(jnp.int32, (8, SIZE), 1)
    sub = lax.broadcasted_iota(jnp.int32, (8, SIZE), 0)
    done = []
    for k in range(count):
        base = 8 * k
        inside = (lane >= base) & (lane < base + 8)
        cols = {(q, i): spread(rows[i][:, base + q : base + q + 1]) for i in range(k, count) for q in range(8)}
        s = {(r, q): spread(cols[q, k][r : r + 1, :]) for r in range(8) for q in range(r + 1)}
        own = jnp.where(inside, jnp.where(lane == base + sub, 1.0, 0.0), rows[k])
        row = [spread(own[q : q + 1, :]) for q in range(8)]
        inv = {}
        m = {}
        for j in range(8):
            inv[j] = recip(s[j, j])
            for i in range(j + 1, 8):
                m[i, j] = s[i, j] * inv[j]
            for i in range(j + 1, 8):
                for t in range(j + 1, i + 1):
                    term = (s[i, j] * s[t, j]) * inv[j] if i == t else m[i, j] * s[t, j]
                    s[i, t] = s[i, t] - term
                row[i] = row[i] - m[i, j] * row[j]
        out = None
        for p in range(8):
            scaled = row[p] * inv_sqrt(s[p, p])
            out = scaled if out is None else jnp.where(sub == p, scaled, out)
        done.append(jnp.where(lane <= base + sub, out, 0.0))
        z = [row[p] * inv[p] for p in range(8)]
        for q in range(6, -1, -1):
            for p in range(7, q, -1):
                z[q] = z[q] - m[p, q] * z[p]
        for i in range(k + 1, count):
            rows[i] = jnp.where(inside, 0.0, rows[i]) - tree_sum([cols[q, i] * z[q] for q in range(8)])
    return done


def split3(value):
    high = value.astype(BF)
    rest = value - high.astype(F32)
    mid = rest.astype(BF)
    return high, mid, (rest - mid.astype(F32)).astype(BF)


def factor_kernel(place, mine, other, high_ref, low_ref, w, diag, following, left, right, sems):
    n = 8
    x, core = place[0], place[1]
    at = lambda i: pl.ds(pl.multiple_of(i * SIZE, SIZE), SIZE)
    exact = functools.partial(jnp.dot, preferred_element_type=F32, precision=EXACT)

    def copies(halves):
        return [
            pltpu.make_async_copy(
                halves[m // HALF].at[m % HALF], w.at[pl.ds(SIZE * i, SIZE), pl.ds(SIZE * j, SIZE)], sems.at[m]
            )
            for m, (i, j) in enumerate(PAIRS)
        ]

    @pl.when(core == 0)
    def _():
        for copy in copies([mine, other]):
            copy.start()

    @pl.when(core == 1)
    def _():
        for copy in copies([other, mine]):
            copy.start()

    diag[...] = jnp.zeros(diag.shape, F32)
    left[...] = jnp.zeros(left.shape, BF)
    for copy in copies([mine, other]):
        copy.wait()
    for i in range(1, n):
        w[pl.ds(SIZE * i, SIZE), pl.ds(0, SIZE * i)] = jnp.zeros((SIZE, SIZE * i), F32)
    w[pl.ds(n * SIZE, (n - 1) * SIZE), :] = jnp.zeros(((n - 1) * SIZE, n * SIZE), F32)
    following[...] = w[pl.ds(0, SIZE), pl.ds(0, SIZE)]

    def step(k, _):
        done = eliminate([following[pl.ds(8 * r, 8), :] for r in range(16)])
        p = jnp.maximum(k - 1, 0)
        x_prev = diag[...]
        w[at(p), :] = jnp.where(k > 0, exact(x_prev, w[at(p), :]), w[at(p), :])
        w[at(p), at(p)] = jnp.where(k > 0, x_prev, w[at(p), at(p)])
        high, mid, low = split3(jnp.where(k > 0, w[at(p), :], 0.0))
        for t, v in enumerate((high, mid, low, high, mid, high)):
            right[pl.ds(SIZE * t, SIZE), :] = v
        for c in range(n):
            cut = slice(SIZE * c, SIZE * c + SIZE)
            high_t, mid_t, low_t = high[:, cut].T, mid[:, cut].T, low[:, cut].T
            for t, v in enumerate((high_t, high_t, high_t, mid_t, mid_t, low_t)):
                left[pl.ds(SIZE * c, SIZE), pl.ds(SIZE * t, SIZE)] = v
        for t in range(n - 1):
            w[at(k + t), at(p)] = jnp.zeros((SIZE, SIZE), F32)
        for t in range(n - 1):
            w[at(k + t), :] = w[at(k + t), :] - jnp.dot(left[at(k + t), :], right[...], preferred_element_type=F32)
        for r in range(16):
            diag[pl.ds(8 * r, 8), :] = done[r]
        q = jnp.minimum(k + 1, n - 1)
        ahead = exact(diag[...], w[at(k), at(q)])
        following[...] = w[at(q), at(q)] - exact(ahead.T, ahead)
        return 0

    lax.fori_loop(0, n, step, 0)
    end = pl.ds((n - 1) * SIZE, SIZE)
    w[end, :] = exact(diag[...], w[end, :])
    w[end, end] = diag[...]
    for r in range(2):
        row = 2 * x + r
        for c in range(n):
            column = 2 * lax.rem(x + c // 2, 4) + c % 2
            value = jnp.where(column <= row, w[at(row), at(column)], 0.0)
            value = value.T
            high = value.astype(BF)
            high_ref[pl.ds(SIZE * c, SIZE), pl.ds(SIZE * r, SIZE)] = high
            low_ref[pl.ds(SIZE * c, SIZE), pl.ds(SIZE * r, SIZE)] = (value - high.astype(F32)).astype(BF)


def factor(place, mine, other):
    n = 8
    vmem = pl.BlockSpec(memory_space=pltpu.VMEM)
    return pl.pallas_call(
        factor_kernel,
        out_shape=[jax.ShapeDtypeStruct((n * SIZE, 2 * SIZE), BF)] * 2,
        grid_spec=pltpu.PrefetchScalarGridSpec(
            num_scalar_prefetch=1,
            grid=(),
            in_specs=[ANY] * 2,
            out_specs=[vmem] * 2,
            scratch_shapes=[
                pltpu.VMEM(((2 * n - 1) * SIZE, n * SIZE), F32),
                pltpu.VMEM((SIZE, SIZE), F32),
                pltpu.VMEM((SIZE, SIZE), F32),
                pltpu.VMEM(((2 * n - 1) * SIZE, 6 * SIZE), BF),
                pltpu.VMEM((6 * SIZE, n * SIZE), BF),
                pltpu.SemaphoreType.DMA((len(PAIRS),)),
            ],
        ),
        compiler_params=params(32),
        cost_estimate=pl.CostEstimate(flops=1_000_000, bytes_accessed=4 * MIB, transcendentals=0),
        name="factor",
    )(place, mine, other)


def apply_kernel(place, *refs):
    own, got, far = refs[0:4], refs[4:7], refs[7:10]
    high, low, out, tiles, sems = refs[10:]
    x = place[0]
    t = pl.program_id(0)
    steps = pl.num_programs(0)
    per = own[0].shape[0]
    width = own[0].shape[-1]
    slot = lax.rem(t, 2)

    def copies(slot, t):
        return [
            pltpu.make_async_copy(
                tiles.at[slot, s], out.at[lax.rem(x + 4 - s, 4), pl.ds(t * per, per)], sems.at[slot, s]
            )
            for s in range(4)
        ]

    @pl.when(t >= 2)
    def _():
        for copy in copies(slot, t - 2):
            copy.wait()

    tall = []
    for s in range(4):
        if s == 0:
            panels = [own[0][...], got[2][...], got[1][...], got[0][...]]
        else:
            panels = [own[4 - s][...]] + [far[s - 1][r] for r in range(3)]
        tall.append(jnp.concatenate([p.reshape(per * SIZE, width) for p in panels], axis=1))
    left = jnp.concatenate(tall, axis=0)
    value = jnp.dot(left, high[...], preferred_element_type=F32)
    value = value + jnp.dot(left, low[...], preferred_element_type=F32)
    tiles[slot] = value.reshape(4, per, SIZE, width)
    for copy in copies(slot, t):
        copy.start()

    @pl.when(t == steps - 1)
    def _():
        for copy in copies(1 - slot, t - 1) + copies(slot, t):
            copy.wait()


def apply(place, own, got, far, high, low):
    width = own[0].shape[-1]
    per = 2
    whole = pl.BlockSpec(high.shape, lambda t, *_: (0, 0))
    rows = pl.BlockSpec((per, SIZE, width), lambda t, *_: (t, 0, 0))
    return pl.pallas_call(
        apply_kernel,
        out_shape=jax.ShapeDtypeStruct((4, 8, SIZE, width), F32),
        grid_spec=pltpu.PrefetchScalarGridSpec(
            num_scalar_prefetch=1,
            grid=(8 // per,),
            in_specs=[rows] * 7 + [pl.BlockSpec((3, per, SIZE, width), lambda t, *_: (0, t, 0, 0))] * 3 + [whole, whole],
            out_specs=ANY,
            scratch_shapes=[pltpu.VMEM((2, 4, per, SIZE, width), F32), pltpu.SemaphoreType.DMA((2, 4))],
        ),
        compiler_params=params(60),
        cost_estimate=pl.CostEstimate(flops=4 * 1024 * 1024 * 256 * 4, bytes_accessed=14 * MIB, transcendentals=0),
        name="apply",
    )(place, *own, *got, *far, high, low)


def shards(vectors, blocks, columns):
    block_rows = blocks.shape[0]
    width = vectors.shape[1]
    row = lax.axis_index("rows")
    x = lax.axis_index("vecs")
    vecs = lax.axis_size("vecs")
    total_rows = vectors.shape[0] * lax.axis_size("rows")
    idx = columns - row * block_rows + REACH
    place = jnp.stack([x, lax.rem(row, 2)]).astype(jnp.int32)
    own = chebyshev(vectors.reshape(block_rows, SIZE, width), blocks, idx, place)
    shift = lambda a, s: lax.ppermute(a, "vecs", [(i, (i + s) % vecs) for i in range(vecs)])
    got = [shift(own[s], s) for s in range(1, vecs)]
    keep, send, *following = gram(total_rows, place, own[0], got)
    mine, other, part = sum_everywhere(keep, send)
    far = [shift(following[s - 1], s) for s in range(1, vecs)]
    inverse_high, inverse_low = factor(place, mine, other)
    return apply(place, own, got, far, inverse_high, inverse_low).reshape(vectors.shape)


def solution(mesh):
    in_specs = (P("rows", "vecs"), P("rows", None, None, None), P("rows", None))
    out_specs = P("rows", "vecs")
    return jax.shard_map(shards, mesh=mesh, in_specs=in_specs, out_specs=out_specs, check_vma=False)
```

```python
import functools

import jax
import jax.numpy as jnp
from jax import lax
from jax.experimental import pallas as pl
from jax.experimental.pallas import tpu as pltpu
from jax.sharding import PartitionSpec as P

DEGREE = 4
filter_center = 0.25
filter_radius = 1.25

F32 = jnp.float32
BF = jnp.bfloat16
EXACT = lax.Precision.HIGHEST
SIZE = 128
REACH = 8
MIB = 1 << 20

ANY = pl.BlockSpec(memory_space=pl.ANY)


def params(mib):
    return pltpu.CompilerParams(vmem_limit_bytes=mib * MIB)


def load_all(pairs, sems):
    copies = [pltpu.make_async_copy(src, dst, sems.at[n]) for n, (src, dst) in enumerate(pairs)]
    for copy in copies:
        copy.start()
    for copy in copies:
        copy.wait()


def row_product(idx, row, shift, blocks_ref, r, pad):
    count = blocks_ref.shape[1]
    left = jnp.concatenate([blocks_ref[r, j] for j in range(count)], axis=1)
    right = jnp.concatenate([pad[idx[row, j] - shift] for j in range(count)], axis=0)
    return jnp.dot(left, right, preferred_element_type=F32)


def recurrence(step, product, current, older):
    scale = (2.0 if step else 1.0) / filter_radius
    newer = scale * product - (scale * filter_center) * current.astype(F32)
    return newer - older.astype(F32) if step else newer


def far_kernel(step, last, whole, idx, place, *refs):
    refs = list(refs)
    take = lambda n: [refs.pop(0) for _ in range(n)]
    blocks, halo, far, mid, current = take(5)
    older = take(1)[0] if step else None
    if last:
        near_new, mid_new = take(2)
        sends = take(4)
        pad, rounded, out_sems = take(3)
    else:
        fresh, rounded, pad = take(3)
    core = place[1]
    first = 24 * core
    far_at = first if whole else 0
    mid_at = (8 if whole else 0) + 8 * core
    pad[pl.ds(16 * core, 8)] = halo[...]
    pad[pl.ds(8, 8)] = far[pl.ds(far_at, 8)]
    pad[pl.ds(16 * (1 - core), 8)] = mid[pl.ds(mid_at, 8)]
    for r in range(8):
        product = row_product(idx, first + r, first, blocks, first + r, pad)
        newer = recurrence(step, product, current[far_at + r], older[(first if step == 1 else 0) + r] if step else None)
        if not last:
            fresh[r] = newer
        rounded[r] = newer.astype(BF)

    if last:
        halves = [mid_new.at[pl.ds(0, 8)], mid_new.at[pl.ds(8, 8)]]
        sources = {0: [rounded] + halves + [near_new], 1: [near_new] + halves + [rounded]}
        for s in range(4):
            for q in range(4):
                for c in range(2):

                    @pl.when((lax.rem(place[0] + s, 4) == q) & (core == c))
                    def _():
                        pltpu.make_async_copy(sources[c][q], sends[s], out_sems.at[s]).start()

        for s in range(4):
            pltpu.make_async_copy(rounded, sends[s], out_sems.at[s]).wait()


def rest_kernel(step, last, whole, idx, place, *refs):
    refs = list(refs)
    take = lambda n: [refs.pop(0) for _ in range(n)]
    blocks, halo, near, mid, far = take(5)
    current = take(2)
    older = take(2) if step else None
    fresh = None if last else take(2)
    rounded = take(2)
    (pad,) = take(1)
    core = place[1]
    near_at = 24 * (1 - core)
    far_at = 24 * core
    pad[pl.ds(40 * (1 - core), 8)] = halo[...]
    pad[pl.ds(8 + near_at, 8)] = near[pl.ds(near_at if whole else 0, 8)]
    pad[pl.ds(16, 16)] = mid[pl.ds(8 if whole else 0, 16)]
    pad[pl.ds(8 + far_at, 8)] = far[pl.ds(far_at if whole else 0, 8)]
    for n, (first, count) in enumerate(((near_at, 8), (8, 16))):
        for r in range(count):
            product = row_product(idx, first + r, 0, blocks, first + r, pad)
            now = current[n][(first if whole else 0) + r]
            before = older[n][(first if step == 1 else 0) + r] if step else None
            newer = recurrence(step, product, now, before)
            if not last:
                fresh[n][r] = newer
            rounded[n][r] = newer.astype(BF)


VMEM = pl.BlockSpec(memory_space=pltpu.VMEM)


def filter_call(kernel, name, step, last, whole, idx, place, blocks, window, groups, moved, halo, rounded, current, older, extra):
    width = halo.shape[-1]
    nnz = blocks.shape[1]
    keys = [key for key, _ in groups]
    operands = [blocks, halo] + [rounded[key] for key in moved] + [current[key] for key in keys]
    if step:
        operands += [older[key] for key in keys]
    operands += extra
    kinds = [BF] if last else [F32, BF]
    shapes = [jax.ShapeDtypeStruct((count, SIZE, width), kind) for kind in kinds for _, count in groups]
    out_specs = [VMEM] * len(shapes)
    scratch = [pltpu.VMEM((window, SIZE, width), BF)]
    if extra:
        shapes = [jax.ShapeDtypeStruct((8, SIZE, width), BF)] * 4
        out_specs = [ANY] * 4
        scratch += [pltpu.VMEM((8, SIZE, width), BF), pltpu.SemaphoreType.DMA((4,))]
    total = sum(count for _, count in groups)
    return pl.pallas_call(
        functools.partial(kernel, step, last, whole),
        out_shape=shapes,
        grid_spec=pltpu.PrefetchScalarGridSpec(
            num_scalar_prefetch=2,
            grid=(),
            in_specs=[VMEM] * len(operands),
            out_specs=out_specs,
            scratch_shapes=scratch,
        ),
        compiler_params=params(16),
        cost_estimate=pl.CostEstimate(
            flops=total * nnz * 2 * SIZE * SIZE * width, bytes_accessed=total * MIB // 2, transcendentals=0
        ),
        name=name,
    )(idx, place, *operands)


def chebyshev(vectors, blocks, idx, place):
    rows = lax.axis_size("rows")
    core = place[1]
    within = [(i, i ^ 1) for i in range(rows)]
    between = [(i, i + 1 if i % 2 else i - 1) for i in range(1, rows - 1)]
    start = dict(near=vectors, mid=vectors, far=vectors)
    rounded = current = start
    older = None
    far_out = lax.dynamic_slice_in_dim(vectors, 24 * core, 8, 0)
    near_out = lax.dynamic_slice_in_dim(vectors, 24 * (1 - core), 8, 0)
    for step in range(DEGREE):
        last = step == DEGREE - 1
        far_halo = lax.ppermute(far_out, "rows", between)
        near_halo = lax.ppermute(near_out, "rows", within)
        common = (step, last, step == 0, idx, place)
        rest = filter_call(
            rest_kernel, "filter_rest", *common, blocks, 48, [("near", 8), ("mid", 16)], ["near", "mid", "far"], near_halo,
            rounded, current, older, [],
        )
        far = filter_call(
            far_kernel, "filter_far", *common, blocks, 24, [("far", 8)], ["far", "mid"], far_halo,
            rounded, current, older, list(rest) if last else [],
        )
        if last:
            return far
        older = current
        current = dict(near=rest[0], mid=rest[1], far=far[0])
        rounded = dict(near=rest[2], mid=rest[3], far=far[1])
        near_out, far_out = rounded["near"], rounded["far"]


PAIRS = [(i, j) for i in range(8) for j in range(i, 8)]
HALF = len(PAIRS) // 2


def gram_kernel(total_rows, place, own, got1, got2, got3, keep, send, first1, first3, next1, next2, next3, f, g, sems, out_sems):
    pieces = [own, got1, got2, got3]
    x, core = place[0], place[1]
    load_all([(pieces[s], f.at[lax.rem(x + 4 - s, 4)]) for s in range(4)], sems)
    places = {
        1: [first1, next1.at[0], next1.at[1]],
        2: [next2.at[0], next2.at[1], next2.at[2]],
        3: [first3, next3.at[0], next3.at[1]],
    }
    copies = [
        pltpu.make_async_copy(f.at[lax.rem(x + s + r, 4)], places[s][r - 1], out_sems.at[3 * s + r - 2])
        for s in (1, 2, 3)
        for r in (1, 2, 3)
    ]
    for copy in copies:
        copy.start()
    depth = 8 * SIZE
    width = f.shape[-1]
    for a in range(4):
        left = f[a].reshape(depth, width).T
        for b in range(a, 4):
            tile = jnp.dot(left, f[b].reshape(depth, width), preferred_element_type=F32) * (1.0 / total_rows)
            for i in range(2):
                for j in range(2):
                    if 2 * a + i <= 2 * b + j:
                        n = PAIRS.index((2 * a + i, 2 * b + j))
                        g[n // HALF, n % HALF] = tile[i * SIZE : (i + 1) * SIZE, j * SIZE : (j + 1) * SIZE]
    copies.append(pltpu.make_async_copy(g.at[core], keep, out_sems.at[0]))
    copies.append(pltpu.make_async_copy(g.at[1 - core], send, out_sems.at[1]))
    for copy in copies[-2:]:
        copy.start()
    for copy in copies:
        copy.wait()


def gram(total_rows, place, own, got):
    width = own.shape[-1]
    half = jax.ShapeDtypeStruct((HALF, SIZE, SIZE), F32)
    return pl.pallas_call(
        functools.partial(gram_kernel, total_rows),
        out_shape=[half, half]
        + [jax.ShapeDtypeStruct((8, SIZE, width), BF)] * 2
        + [jax.ShapeDtypeStruct((n, 8, SIZE, width), BF) for n in (2, 3, 2)],
        grid_spec=pltpu.PrefetchScalarGridSpec(
            num_scalar_prefetch=1,
            grid=(),
            in_specs=[ANY] * 4,
            out_specs=[ANY] * 7,
            scratch_shapes=[
                pltpu.VMEM((4, 8, SIZE, width), BF),
                pltpu.VMEM((2, HALF, SIZE, SIZE), F32),
                pltpu.SemaphoreType.DMA((4,)),
                pltpu.SemaphoreType.DMA((11,)),
            ],
        ),
        compiler_params=params(16),
        cost_estimate=pl.CostEstimate(flops=10 * 2 * 1024 * 256 * 256, bytes_accessed=8 * MIB, transcendentals=0),
        name="gram",
    )(place, own, *got)


def sum_everywhere(keep, send, first):
    rows = lax.axis_size("rows")
    vecs = lax.axis_size("vecs")
    swap = [(i, i ^ 1) for i in range(rows)]
    groups = [list(range(c, rows, 2)) for c in range(2)]
    count = rows // 2
    mine = keep + lax.ppermute(send, "rows", swap)
    parts = mine.reshape(count, -1, mine.shape[-1])
    parts = lax.all_to_all(parts, "rows", 0, 0, axis_index_groups=groups, tiled=True)
    part = jnp.sum(parts, axis=0)
    part, *first = lax.optimization_barrier((part, *first))
    others = [lax.ppermute(part, "vecs", [(i, (i + s) % vecs) for i in range(vecs)]) for s in range(1, vecs)]
    part = part + sum(others)
    spread_out = jnp.broadcast_to(part[None], (count,) + part.shape)
    mine = lax.all_to_all(spread_out, "rows", 0, 0, axis_index_groups=groups, tiled=True).reshape(keep.shape)
    return mine, lax.ppermute(mine, "rows", swap), first


def recip(x):
    return pl.reciprocal(x, approx=True)


def inv_sqrt(x):
    y = lax.rsqrt(x)
    return y * (1.5 - 0.5 * x * (y * y))


def spread(x):
    return jnp.broadcast_to(x, (8, SIZE))


def tree_sum(terms):
    while len(terms) > 1:
        terms = [terms[i] + terms[i + 1] if i + 1 < len(terms) else terms[i] for i in range(0, len(terms), 2)]
    return terms[0]


def eliminate(rows):
    count = len(rows)
    lane = lax.broadcasted_iota(jnp.int32, (8, SIZE), 1)
    sub = lax.broadcasted_iota(jnp.int32, (8, SIZE), 0)
    done = []
    for k in range(count):
        base = 8 * k
        inside = (lane >= base) & (lane < base + 8)
        cols = {(q, i): spread(rows[i][:, base + q : base + q + 1]) for i in range(k, count) for q in range(8)}
        s = {(r, q): spread(cols[q, k][r : r + 1, :]) for r in range(8) for q in range(r + 1)}
        own = jnp.where(inside, jnp.where(lane == base + sub, 1.0, 0.0), rows[k])
        row = [spread(own[q : q + 1, :]) for q in range(8)]
        inv = {}
        m = {}
        for j in range(8):
            inv[j] = recip(s[j, j])
            for i in range(j + 1, 8):
                m[i, j] = s[i, j] * inv[j]
            for i in range(j + 1, 8):
                for t in range(j + 1, i + 1):
                    term = (s[i, j] * s[t, j]) * inv[j] if i == t else m[i, j] * s[t, j]
                    s[i, t] = s[i, t] - term
                row[i] = row[i] - m[i, j] * row[j]
        out = None
        for p in range(8):
            scaled = row[p] * inv_sqrt(s[p, p])
            out = scaled if out is None else jnp.where(sub == p, scaled, out)
        done.append(jnp.where(lane <= base + sub, out, 0.0))
        z = [row[p] * inv[p] for p in range(8)]
        for q in range(6, -1, -1):
            for p in range(7, q, -1):
                z[q] = z[q] - m[p, q] * z[p]
        for i in range(k + 1, count):
            rows[i] = jnp.where(inside, 0.0, rows[i]) - tree_sum([cols[q, i] * z[q] for q in range(8)])
    return done


def split3(value):
    high = value.astype(BF)
    rest = value - high.astype(F32)
    mid = rest.astype(BF)
    return high, mid, (rest - mid.astype(F32)).astype(BF)


def factor_kernel(place, mine, other, *refs):
    arrays, (high_ref, low_ref, held, w, diag, following, left, right, sems, held_sems) = refs[:9], refs[9:]
    n = 8
    x, core = place[0], place[1]
    bring = [pltpu.make_async_copy(array, held.at[m], held_sems.at[m]) for m, array in enumerate(arrays)]
    at = lambda i: pl.ds(pl.multiple_of(i * SIZE, SIZE), SIZE)
    exact = functools.partial(jnp.dot, preferred_element_type=F32, precision=EXACT)

    def copies(halves):
        return [
            pltpu.make_async_copy(
                halves[m // HALF].at[m % HALF], w.at[pl.ds(SIZE * i, SIZE), pl.ds(SIZE * j, SIZE)], sems.at[m]
            )
            for m, (i, j) in enumerate(PAIRS)
        ]

    @pl.when(core == 0)
    def _():
        for copy in copies([mine, other]):
            copy.start()

    @pl.when(core == 1)
    def _():
        for copy in copies([other, mine]):
            copy.start()

    for copy in bring:
        copy.start()
    diag[...] = jnp.zeros(diag.shape, F32)
    left[...] = jnp.zeros(left.shape, BF)
    for copy in copies([mine, other]):
        copy.wait()
    for i in range(1, n):
        w[pl.ds(SIZE * i, SIZE), pl.ds(0, SIZE * i)] = jnp.zeros((SIZE, SIZE * i), F32)
    w[pl.ds(n * SIZE, (n - 1) * SIZE), :] = jnp.zeros(((n - 1) * SIZE, n * SIZE), F32)
    following[...] = w[pl.ds(0, SIZE), pl.ds(0, SIZE)]

    def step(k, _):
        done = eliminate([following[pl.ds(8 * r, 8), :] for r in range(16)])
        p = jnp.maximum(k - 1, 0)
        x_prev = diag[...]
        w[at(p), :] = jnp.where(k > 0, exact(x_prev, w[at(p), :]), w[at(p), :])
        w[at(p), at(p)] = jnp.where(k > 0, x_prev, w[at(p), at(p)])
        high, mid, low = split3(jnp.where(k > 0, w[at(p), :], 0.0))
        for t, v in enumerate((high, mid, low, high, mid, high)):
            right[pl.ds(SIZE * t, SIZE), :] = v
        for c in range(n):
            cut = slice(SIZE * c, SIZE * c + SIZE)
            high_t, mid_t, low_t = high[:, cut].T, mid[:, cut].T, low[:, cut].T
            for t, v in enumerate((high_t, high_t, high_t, mid_t, mid_t, low_t)):
                left[pl.ds(SIZE * c, SIZE), pl.ds(SIZE * t, SIZE)] = v
        for t in range(n - 1):
            w[at(k + t), at(p)] = jnp.zeros((SIZE, SIZE), F32)
        for t in range(n - 1):
            w[at(k + t), :] = w[at(k + t), :] - jnp.dot(left[at(k + t), :], right[...], preferred_element_type=F32)
        for r in range(16):
            diag[pl.ds(8 * r, 8), :] = done[r]
        q = jnp.minimum(k + 1, n - 1)
        ahead = exact(diag[...], w[at(k), at(q)])
        following[...] = w[at(q), at(q)] - exact(ahead.T, ahead)
        return 0

    lax.fori_loop(0, n, step, 0)
    end = pl.ds((n - 1) * SIZE, SIZE)
    w[end, :] = exact(diag[...], w[end, :])
    w[end, end] = diag[...]
    for copy in bring:
        copy.wait()
    for r in range(2):
        row = 2 * x + r
        for c in range(n):
            column = 2 * lax.rem(x + c // 2, 4) + c % 2
            value = jnp.where(column <= row, w[at(row), at(column)], 0.0)
            value = value.T
            high = value.astype(BF)
            high_ref[pl.ds(SIZE * c, SIZE), pl.ds(SIZE * r, SIZE)] = high
            low_ref[pl.ds(SIZE * c, SIZE), pl.ds(SIZE * r, SIZE)] = (value - high.astype(F32)).astype(BF)


def factor(place, mine, other, arrays):
    n = 8
    vmem = pl.BlockSpec(memory_space=pltpu.VMEM)
    return pl.pallas_call(
        factor_kernel,
        out_shape=[jax.ShapeDtypeStruct((n * SIZE, 2 * SIZE), BF)] * 2
        + [jax.ShapeDtypeStruct((len(arrays),) + arrays[0].shape, BF)],
        grid_spec=pltpu.PrefetchScalarGridSpec(
            num_scalar_prefetch=1,
            grid=(),
            in_specs=[ANY] * (2 + len(arrays)),
            out_specs=[vmem] * 3,
            scratch_shapes=[
                pltpu.VMEM(((2 * n - 1) * SIZE, n * SIZE), F32),
                pltpu.VMEM((SIZE, SIZE), F32),
                pltpu.VMEM((SIZE, SIZE), F32),
                pltpu.VMEM(((2 * n - 1) * SIZE, 6 * SIZE), BF),
                pltpu.VMEM((6 * SIZE, n * SIZE), BF),
                pltpu.SemaphoreType.DMA((len(PAIRS),)),
                pltpu.SemaphoreType.DMA((len(arrays),)),
            ],
        ),
        compiler_params=params(24),
        cost_estimate=pl.CostEstimate(flops=1_000_000, bytes_accessed=4 * MIB, transcendentals=0),
        name="factor",
    )(place, mine, other, *arrays)


def apply_kernel(place, *refs):
    held, far1, far2_at, far3, high, low, out, far2, tiles, in_sems, sems = refs
    far = [far1, far2, far3]
    own = [held.at[n] for n in range(4)]
    got = [held.at[n] for n in range(4, 7)]
    near = [held.at[n] for n in range(7, 9)]
    x = place[0]
    count = held.shape[1]
    per = tiles.shape[2]
    width = held.shape[-1]

    def copies(t):
        return [
            pltpu.make_async_copy(
                tiles.at[t % 2, s], out.at[lax.rem(x + 4 - s, 4), pl.ds(t * per, per)], sems.at[t % 2, s]
            )
            for s in range(4)
        ]

    def load(t):
        part = pl.ds(t * per, per)
        return pltpu.make_async_copy(far2_at.at[:, part], far2.at[:, part], in_sems.at[t])

    for t in range(count // per):
        load(t).start()
    for t in range(count // per):
        if t >= 2:
            for copy in copies(t - 2):
                copy.wait()
        rows = slice(t * per, (t + 1) * per)
        for s in (0, 1, 3, 2):
            if s == 2:
                load(t).wait()
            if s == 0:
                panels = [own[0][rows], got[2][rows], got[1][rows], got[0][rows]]
            elif s == 2:
                panels = [own[2][rows]] + [far[1][r, rows] for r in range(3)]
            else:
                panels = [own[4 - s][rows], near[s // 2][rows]] + [far[s - 1][r, rows] for r in range(2)]
            left = jnp.concatenate([p.reshape(per * SIZE, width) for p in panels], axis=1)
            value = jnp.dot(left, high[...], preferred_element_type=F32)
            value = value + jnp.dot(left, low[...], preferred_element_type=F32)
            tiles[t % 2, s] = value.reshape(per, SIZE, width)
        for copy in copies(t):
            copy.start()
    for t in range(count // per - 2, count // per):
        for copy in copies(t):
            copy.wait()


def apply(place, held, far, high, low):
    width = held.shape[-1]
    return pl.pallas_call(
        apply_kernel,
        out_shape=jax.ShapeDtypeStruct((4, 8, SIZE, width), F32),
        grid_spec=pltpu.PrefetchScalarGridSpec(
            num_scalar_prefetch=1,
            grid=(),
            in_specs=[VMEM, VMEM, ANY, VMEM, VMEM, VMEM],
            out_specs=ANY,
            scratch_shapes=[
                pltpu.VMEM(far[1].shape, BF),
                pltpu.VMEM((2, 4, 2, SIZE, width), F32),
                pltpu.SemaphoreType.DMA((4,)),
                pltpu.SemaphoreType.DMA((2, 4)),
            ],
        ),
        compiler_params=params(24),
        cost_estimate=pl.CostEstimate(flops=4 * 1024 * 1024 * 256 * 4, bytes_accessed=14 * MIB, transcendentals=0),
        name="apply",
    )(place, held, *far, high, low)


def shards(vectors, blocks, columns):
    block_rows = blocks.shape[0]
    width = vectors.shape[1]
    row = lax.axis_index("rows")
    x = lax.axis_index("vecs")
    vecs = lax.axis_size("vecs")
    total_rows = vectors.shape[0] * lax.axis_size("rows")
    idx = columns - row * block_rows + REACH
    place = jnp.stack([x, lax.rem(row, 2)]).astype(jnp.int32)
    own = chebyshev(vectors.reshape(block_rows, SIZE, width), blocks, idx, place)
    shift = lambda a, s: lax.ppermute(a, "vecs", [(i, (i + s) % vecs) for i in range(vecs)])
    got = [shift(own[s], s) for s in range(1, vecs)]
    keep, send, first1, first3, *following = gram(total_rows, place, own[0], got)
    near = [shift(first1, 1), shift(first3, 3)]
    mine, other, near = sum_everywhere(keep, send, near)
    far = [shift(following[s - 1], s) for s in range(1, vecs)]
    inverse_high, inverse_low, held = factor(place, mine, other, [*own, *got, *near])
    return apply(place, held, far, inverse_high, inverse_low).reshape(vectors.shape)


def solution(mesh):
    in_specs = (P("rows", "vecs"), P("rows", None, None, None), P("rows", None))
    out_specs = P("rows", "vecs")
    return jax.shard_map(shards, mesh=mesh, in_specs=in_specs, out_specs=out_specs, check_vma=False)
```

```python
import functools

import jax
import jax.numpy as jnp
from jax import lax
from jax.experimental import pallas as pl
from jax.experimental.pallas import tpu as pltpu
from jax.sharding import PartitionSpec as P

DEGREE = 4
filter_center = 0.25
filter_radius = 1.25

F32 = jnp.float32
BF = jnp.bfloat16
EXACT = lax.Precision.HIGHEST
SIZE = 128
REACH = 8
MIB = 1 << 20

ANY = pl.BlockSpec(memory_space=pl.ANY)


def params(mib):
    return pltpu.CompilerParams(vmem_limit_bytes=mib * MIB)


def load_all(pairs, sems):
    copies = [pltpu.make_async_copy(src, dst, sems.at[n]) for n, (src, dst) in enumerate(pairs)]
    for copy in copies:
        copy.start()
    for copy in copies:
        copy.wait()


def row_product(idx, row, shift, blocks_ref, r, pad):
    count = blocks_ref.shape[1]
    left = jnp.concatenate([blocks_ref[r, j] for j in range(count)], axis=1)
    right = jnp.concatenate([pad[idx[row, j] - shift] for j in range(count)], axis=0)
    return jnp.dot(left, right, preferred_element_type=F32)


def recurrence(step, product, current, older):
    scale = (2.0 if step else 1.0) / filter_radius
    newer = scale * product - (scale * filter_center) * current.astype(F32)
    return newer - older.astype(F32) if step else newer


def far_kernel(step, last, whole, idx, place, *refs):
    refs = list(refs)
    take = lambda n: [refs.pop(0) for _ in range(n)]
    blocks, halo, far, mid, current = take(5)
    older = take(1)[0] if step else None
    if last:
        near_new, mid_new = take(2)
        sends = take(4)
        pad, rounded, out_sems = take(3)
    else:
        fresh, rounded, pad = take(3)
    core = place[1]
    first = 24 * core
    far_at = first if whole else 0
    mid_at = (8 if whole else 0) + 8 * core
    pad[pl.ds(16 * core, 8)] = halo[...]
    pad[pl.ds(8, 8)] = far[pl.ds(far_at, 8)]
    pad[pl.ds(16 * (1 - core), 8)] = mid[pl.ds(mid_at, 8)]
    for r in range(8):
        product = row_product(idx, first + r, first, blocks, first + r, pad)
        newer = recurrence(step, product, current[far_at + r], older[(first if step == 1 else 0) + r] if step else None)
        if not last:
            fresh[r] = newer
        rounded[r] = newer.astype(BF)

    if last:
        halves = [mid_new.at[pl.ds(0, 8)], mid_new.at[pl.ds(8, 8)]]
        sources = {0: [rounded] + halves + [near_new], 1: [near_new] + halves + [rounded]}
        for s in range(4):
            for q in range(4):
                for c in range(2):

                    @pl.when((lax.rem(place[0] + s, 4) == q) & (core == c))
                    def _():
                        pltpu.make_async_copy(sources[c][q], sends[s], out_sems.at[s]).start()

        for s in range(4):
            pltpu.make_async_copy(rounded, sends[s], out_sems.at[s]).wait()


def rest_kernel(step, last, whole, idx, place, *refs):
    refs = list(refs)
    take = lambda n: [refs.pop(0) for _ in range(n)]
    blocks, halo, near, mid, far = take(5)
    current = take(2)
    older = take(2) if step else None
    fresh = None if last else take(2)
    rounded = take(2)
    (pad,) = take(1)
    core = place[1]
    near_at = 24 * (1 - core)
    far_at = 24 * core
    pad[pl.ds(40 * (1 - core), 8)] = halo[...]
    pad[pl.ds(8 + near_at, 8)] = near[pl.ds(near_at if whole else 0, 8)]
    pad[pl.ds(16, 16)] = mid[pl.ds(8 if whole else 0, 16)]
    pad[pl.ds(8 + far_at, 8)] = far[pl.ds(far_at if whole else 0, 8)]
    for n, (first, count) in enumerate(((near_at, 8), (8, 16))):
        for r in range(count):
            product = row_product(idx, first + r, 0, blocks, first + r, pad)
            now = current[n][(first if whole else 0) + r]
            before = older[n][(first if step == 1 else 0) + r] if step else None
            newer = recurrence(step, product, now, before)
            if not last:
                fresh[n][r] = newer
            rounded[n][r] = newer.astype(BF)


VMEM = pl.BlockSpec(memory_space=pltpu.VMEM)


def filter_call(kernel, name, step, last, whole, idx, place, blocks, window, groups, moved, halo, rounded, current, older, extra):
    width = halo.shape[-1]
    nnz = blocks.shape[1]
    keys = [key for key, _ in groups]
    operands = [blocks, halo] + [rounded[key] for key in moved] + [current[key] for key in keys]
    if step:
        operands += [older[key] for key in keys]
    operands += extra
    kinds = [BF] if last else [F32, BF]
    shapes = [jax.ShapeDtypeStruct((count, SIZE, width), kind) for kind in kinds for _, count in groups]
    out_specs = [VMEM] * len(shapes)
    scratch = [pltpu.VMEM((window, SIZE, width), BF)]
    if extra:
        shapes = [jax.ShapeDtypeStruct((8, SIZE, width), BF)] * 4
        out_specs = [ANY] * 4
        scratch += [pltpu.VMEM((8, SIZE, width), BF), pltpu.SemaphoreType.DMA((4,))]
    total = sum(count for _, count in groups)
    return pl.pallas_call(
        functools.partial(kernel, step, last, whole),
        out_shape=shapes,
        grid_spec=pltpu.PrefetchScalarGridSpec(
            num_scalar_prefetch=2,
            grid=(),
            in_specs=[VMEM] * len(operands),
            out_specs=out_specs,
            scratch_shapes=scratch,
        ),
        compiler_params=params(30),
        cost_estimate=pl.CostEstimate(
            flops=total * nnz * 2 * SIZE * SIZE * width, bytes_accessed=total * MIB // 2, transcendentals=0
        ),
        name=name,
    )(idx, place, *operands)


def chebyshev(vectors, blocks, idx, place):
    rows = lax.axis_size("rows")
    core = place[1]
    within = [(i, i ^ 1) for i in range(rows)]
    between = [(i, i + 1 if i % 2 else i - 1) for i in range(1, rows - 1)]
    start = dict(near=vectors, mid=vectors, far=vectors)
    rounded = current = start
    older = None
    far_out = lax.dynamic_slice_in_dim(vectors, 24 * core, 8, 0)
    near_out = lax.dynamic_slice_in_dim(vectors, 24 * (1 - core), 8, 0)
    for step in range(DEGREE):
        last = step == DEGREE - 1
        far_halo = lax.ppermute(far_out, "rows", between)
        near_halo = lax.ppermute(near_out, "rows", within)
        common = (step, last, step == 0, idx, place)
        rest = filter_call(
            rest_kernel, "filter_rest", *common, blocks, 48, [("near", 8), ("mid", 16)], ["near", "mid", "far"], near_halo,
            rounded, current, older, [],
        )
        far = filter_call(
            far_kernel, "filter_far", *common, blocks, 24, [("far", 8)], ["far", "mid"], far_halo,
            rounded, current, older, list(rest) if last else [],
        )
        if last:
            return far
        older = current
        current = dict(near=rest[0], mid=rest[1], far=far[0])
        rounded = dict(near=rest[2], mid=rest[3], far=far[1])
        near_out, far_out = rounded["near"], rounded["far"]


PAIRS = [(i, j) for i in range(8) for j in range(i, 8)]
HALF = len(PAIRS) // 2


def gram_kernel(total_rows, place, own, got1, got2, got3, keep, send, next1, next2, next3, f, g, sems, out_sems):
    pieces = [own, got1, got2, got3]
    x, core = place[0], place[1]
    load_all([(pieces[s], f.at[lax.rem(x + 4 - s, 4)]) for s in range(4)], sems)
    copies = [
        pltpu.make_async_copy(f.at[lax.rem(x + s + r, 4)], out.at[r - 1], out_sems.at[3 * s + r - 2])
        for s, out in ((1, next1), (2, next2), (3, next3))
        for r in (1, 2, 3)
    ]
    for copy in copies:
        copy.start()
    depth = 8 * SIZE
    width = f.shape[-1]
    for a in range(4):
        left = f[a].reshape(depth, width).T
        for b in range(a, 4):
            tile = jnp.dot(left, f[b].reshape(depth, width), preferred_element_type=F32) * (1.0 / total_rows)
            for i in range(2):
                for j in range(2):
                    if 2 * a + i <= 2 * b + j:
                        n = PAIRS.index((2 * a + i, 2 * b + j))
                        g[n // HALF, n % HALF] = tile[i * SIZE : (i + 1) * SIZE, j * SIZE : (j + 1) * SIZE]
    copies.append(pltpu.make_async_copy(g.at[core], keep, out_sems.at[0]))
    copies.append(pltpu.make_async_copy(g.at[1 - core], send, out_sems.at[1]))
    for copy in copies[-2:]:
        copy.start()
    for copy in copies:
        copy.wait()


def gram(total_rows, place, own, got):
    width = own.shape[-1]
    half = jax.ShapeDtypeStruct((HALF, SIZE, SIZE), F32)
    return pl.pallas_call(
        functools.partial(gram_kernel, total_rows),
        out_shape=[half, half] + [jax.ShapeDtypeStruct((3, 8, SIZE, width), BF)] * 3,
        grid_spec=pltpu.PrefetchScalarGridSpec(
            num_scalar_prefetch=1,
            grid=(),
            in_specs=[ANY] * 4,
            out_specs=[ANY] * 5,
            scratch_shapes=[
                pltpu.VMEM((4, 8, SIZE, width), BF),
                pltpu.VMEM((2, HALF, SIZE, SIZE), F32),
                pltpu.SemaphoreType.DMA((4,)),
                pltpu.SemaphoreType.DMA((11,)),
            ],
        ),
        compiler_params=params(24),
        cost_estimate=pl.CostEstimate(flops=10 * 2 * 1024 * 256 * 256, bytes_accessed=8 * MIB, transcendentals=0),
        name="gram",
    )(place, own, *got)


def sum_everywhere(keep, send):
    rows = lax.axis_size("rows")
    vecs = lax.axis_size("vecs")
    swap = [(i, i ^ 1) for i in range(rows)]
    groups = [list(range(c, rows, 2)) for c in range(2)]
    count = rows // 2
    mine = keep + lax.ppermute(send, "rows", swap)
    parts = mine.reshape(count, -1, mine.shape[-1])
    parts = lax.all_to_all(parts, "rows", 0, 0, axis_index_groups=groups, tiled=True)
    part = jnp.sum(parts, axis=0)
    others = [lax.ppermute(part, "vecs", [(i, (i + s) % vecs) for i in range(vecs)]) for s in range(1, vecs)]
    spread_out = sum(jnp.broadcast_to(p[None], (count,) + p.shape) for p in [part] + others)
    mine = lax.all_to_all(spread_out, "rows", 0, 0, axis_index_groups=groups, tiled=True).reshape(keep.shape)
    return mine, lax.ppermute(mine, "rows", swap)


def recip(x):
    return pl.reciprocal(x, approx=True)


def inv_sqrt(x):
    y = lax.rsqrt(x)
    return y * (1.5 - 0.5 * x * (y * y))


def spread(x):
    return jnp.broadcast_to(x, (8, SIZE))


def tree_sum(terms):
    while len(terms) > 1:
        terms = [terms[i] + terms[i + 1] if i + 1 < len(terms) else terms[i] for i in range(0, len(terms), 2)]
    return terms[0]


def eliminate(rows):
    count = len(rows)
    lane = lax.broadcasted_iota(jnp.int32, (8, SIZE), 1)
    sub = lax.broadcasted_iota(jnp.int32, (8, SIZE), 0)
    done = []
    for k in range(count):
        base = 8 * k
        inside = (lane >= base) & (lane < base + 8)
        cols = {(q, i): spread(rows[i][:, base + q : base + q + 1]) for i in range(k, count) for q in range(8)}
        s = {(r, q): spread(cols[q, k][r : r + 1, :]) for r in range(8) for q in range(r + 1)}
        own = jnp.where(inside, jnp.where(lane == base + sub, 1.0, 0.0), rows[k])
        row = [spread(own[q : q + 1, :]) for q in range(8)]
        inv = {}
        m = {}
        for j in range(8):
            inv[j] = recip(s[j, j])
            for i in range(j + 1, 8):
                m[i, j] = s[i, j] * inv[j]
            for i in range(j + 1, 8):
                for t in range(j + 1, i + 1):
                    term = (s[i, j] * s[t, j]) * inv[j] if i == t else m[i, j] * s[t, j]
                    s[i, t] = s[i, t] - term
                row[i] = row[i] - m[i, j] * row[j]
        out = None
        for p in range(8):
            scaled = row[p] * inv_sqrt(s[p, p])
            out = scaled if out is None else jnp.where(sub == p, scaled, out)
        done.append(jnp.where(lane <= base + sub, out, 0.0))
        z = [row[p] * inv[p] for p in range(8)]
        for q in range(6, -1, -1):
            for p in range(7, q, -1):
                z[q] = z[q] - m[p, q] * z[p]
        for i in range(k + 1, count):
            rows[i] = jnp.where(inside, 0.0, rows[i]) - tree_sum([cols[q, i] * z[q] for q in range(8)])
    return done


def split3(value):
    high = value.astype(BF)
    rest = value - high.astype(F32)
    mid = rest.astype(BF)
    return high, mid, (rest - mid.astype(F32)).astype(BF)


def factor_kernel(place, mine, other, high_ref, low_ref, w, diag, following, left, right, sems):
    n = 8
    x, core = place[0], place[1]
    at = lambda i: pl.ds(pl.multiple_of(i * SIZE, SIZE), SIZE)
    exact = functools.partial(jnp.dot, preferred_element_type=F32, precision=EXACT)

    def copies(halves):
        return [
            pltpu.make_async_copy(
                halves[m // HALF].at[m % HALF], w.at[pl.ds(SIZE * i, SIZE), pl.ds(SIZE * j, SIZE)], sems.at[m]
            )
            for m, (i, j) in enumerate(PAIRS)
        ]

    @pl.when(core == 0)
    def _():
        for copy in copies([mine, other]):
            copy.start()

    @pl.when(core == 1)
    def _():
        for copy in copies([other, mine]):
            copy.start()

    diag[...] = jnp.zeros(diag.shape, F32)
    left[...] = jnp.zeros(left.shape, BF)
    for copy in copies([mine, other]):
        copy.wait()
    for i in range(1, n):
        w[pl.ds(SIZE * i, SIZE), pl.ds(0, SIZE * i)] = jnp.zeros((SIZE, SIZE * i), F32)
    w[pl.ds(n * SIZE, (n - 1) * SIZE), :] = jnp.zeros(((n - 1) * SIZE, n * SIZE), F32)
    following[...] = w[pl.ds(0, SIZE), pl.ds(0, SIZE)]

    def step(k, _):
        done = eliminate([following[pl.ds(8 * r, 8), :] for r in range(16)])
        p = jnp.maximum(k - 1, 0)
        x_prev = diag[...]
        w[at(p), :] = jnp.where(k > 0, exact(x_prev, w[at(p), :]), w[at(p), :])
        w[at(p), at(p)] = jnp.where(k > 0, x_prev, w[at(p), at(p)])
        high, mid, low = split3(jnp.where(k > 0, w[at(p), :], 0.0))
        for t, v in enumerate((high, mid, low, high, mid, high)):
            right[pl.ds(SIZE * t, SIZE), :] = v
        for c in range(n):
            cut = slice(SIZE * c, SIZE * c + SIZE)
            high_t, mid_t, low_t = high[:, cut].T, mid[:, cut].T, low[:, cut].T
            for t, v in enumerate((high_t, high_t, high_t, mid_t, mid_t, low_t)):
                left[pl.ds(SIZE * c, SIZE), pl.ds(SIZE * t, SIZE)] = v
        for t in range(n - 1):
            w[at(k + t), at(p)] = jnp.zeros((SIZE, SIZE), F32)
        for t in range(n - 1):
            w[at(k + t), :] = w[at(k + t), :] - jnp.dot(left[at(k + t), :], right[...], preferred_element_type=F32)
        for r in range(16):
            diag[pl.ds(8 * r, 8), :] = done[r]
        q = jnp.minimum(k + 1, n - 1)
        ahead = exact(diag[...], w[at(k), at(q)])
        following[...] = w[at(q), at(q)] - exact(ahead.T, ahead)
        return 0

    lax.fori_loop(0, n, step, 0)
    end = pl.ds((n - 1) * SIZE, SIZE)
    w[end, :] = exact(diag[...], w[end, :])
    w[end, end] = diag[...]
    for r in range(2):
        row = 2 * x + r
        for c in range(n):
            column = 2 * lax.rem(x + c // 2, 4) + c % 2
            value = jnp.where(column <= row, w[at(row), at(column)], 0.0)
            value = value.T
            high = value.astype(BF)
            high_ref[pl.ds(SIZE * c, SIZE), pl.ds(SIZE * r, SIZE)] = high
            low_ref[pl.ds(SIZE * c, SIZE), pl.ds(SIZE * r, SIZE)] = (value - high.astype(F32)).astype(BF)


def factor(place, mine, other):
    n = 8
    vmem = pl.BlockSpec(memory_space=pltpu.VMEM)
    return pl.pallas_call(
        factor_kernel,
        out_shape=[jax.ShapeDtypeStruct((n * SIZE, 2 * SIZE), BF)] * 2,
        grid_spec=pltpu.PrefetchScalarGridSpec(
            num_scalar_prefetch=1,
            grid=(),
            in_specs=[ANY] * 2,
            out_specs=[vmem] * 2,
            scratch_shapes=[
                pltpu.VMEM(((2 * n - 1) * SIZE, n * SIZE), F32),
                pltpu.VMEM((SIZE, SIZE), F32),
                pltpu.VMEM((SIZE, SIZE), F32),
                pltpu.VMEM(((2 * n - 1) * SIZE, 6 * SIZE), BF),
                pltpu.VMEM((6 * SIZE, n * SIZE), BF),
                pltpu.SemaphoreType.DMA((len(PAIRS),)),
            ],
        ),
        compiler_params=params(32),
        cost_estimate=pl.CostEstimate(flops=1_000_000, bytes_accessed=4 * MIB, transcendentals=0),
        name="factor",
    )(place, mine, other)


def apply_kernel(place, *refs):
    own, got, far = refs[0:4], refs[4:7], refs[7:10]
    high, low, out, tiles, sems = refs[10:]
    x = place[0]
    t = pl.program_id(0)
    steps = pl.num_programs(0)
    per = own[0].shape[0]
    width = own[0].shape[-1]
    slot = lax.rem(t, 2)

    def copies(slot, t):
        return [
            pltpu.make_async_copy(
                tiles.at[slot, s], out.at[lax.rem(x + 4 - s, 4), pl.ds(t * per, per)], sems.at[slot, s]
            )
            for s in range(4)
        ]

    @pl.when(t >= 2)
    def _():
        for copy in copies(slot, t - 2):
            copy.wait()

    tall = []
    for s in range(4):
        if s == 0:
            panels = [own[0][...], got[2][...], got[1][...], got[0][...]]
        else:
            panels = [own[4 - s][...]] + [far[s - 1][r] for r in range(3)]
        tall.append(jnp.concatenate([p.reshape(per * SIZE, width) for p in panels], axis=1))
    left = jnp.concatenate(tall, axis=0)
    value = jnp.dot(left, high[...], preferred_element_type=F32)
    value = value + jnp.dot(left, low[...], preferred_element_type=F32)
    tiles[slot] = value.reshape(4, per, SIZE, width)
    for copy in copies(slot, t):
        copy.start()

    @pl.when(t == steps - 1)
    def _():
        for copy in copies(1 - slot, t - 1) + copies(slot, t):
            copy.wait()


def apply(place, own, got, far, high, low):
    width = own[0].shape[-1]
    per = 4
    whole = pl.BlockSpec(high.shape, lambda t, *_: (0, 0))
    rows = pl.BlockSpec((per, SIZE, width), lambda t, *_: (t, 0, 0))
    return pl.pallas_call(
        apply_kernel,
        out_shape=jax.ShapeDtypeStruct((4, 8, SIZE, width), F32),
        grid_spec=pltpu.PrefetchScalarGridSpec(
            num_scalar_prefetch=1,
            grid=(8 // per,),
            in_specs=[rows] * 7 + [pl.BlockSpec((3, per, SIZE, width), lambda t, *_: (0, t, 0, 0))] * 3 + [whole, whole],
            out_specs=ANY,
            scratch_shapes=[pltpu.VMEM((2, 4, per, SIZE, width), F32), pltpu.SemaphoreType.DMA((2, 4))],
        ),
        compiler_params=params(60),
        cost_estimate=pl.CostEstimate(flops=4 * 1024 * 1024 * 256 * 4, bytes_accessed=14 * MIB, transcendentals=0),
        name="apply",
    )(place, *own, *got, *far, high, low)


def shards(vectors, blocks, columns):
    block_rows = blocks.shape[0]
    width = vectors.shape[1]
    row = lax.axis_index("rows")
    x = lax.axis_index("vecs")
    vecs = lax.axis_size("vecs")
    total_rows = vectors.shape[0] * lax.axis_size("rows")
    idx = columns - row * block_rows + REACH
    place = jnp.stack([x, lax.rem(row, 2)]).astype(jnp.int32)
    own = chebyshev(vectors.reshape(block_rows, SIZE, width), blocks, idx, place)
    shift = lambda a, s: lax.ppermute(a, "vecs", [(i, (i + s) % vecs) for i in range(vecs)])
    got = [shift(own[s], s) for s in range(1, vecs)]
    keep, send, *following = gram(total_rows, place, own[0], got)
    mine, other = sum_everywhere(keep, send)
    far = [shift(following[s - 1], s) for s in range(1, vecs)]
    inverse_high, inverse_low = factor(place, mine, other)
    return apply(place, own, got, far, inverse_high, inverse_low).reshape(vectors.shape)


def solution(mesh):
    in_specs = (P("rows", "vecs"), P("rows", None, None, None), P("rows", None))
    out_specs = P("rows", "vecs")
    return jax.shard_map(shards, mesh=mesh, in_specs=in_specs, out_specs=out_specs, check_vma=False)
```
